128 devices in a mesh: dp: 16 (over z, y_lo, core), inner: 8 (over y_hi, x).
Axes of the slice: x: 4, y: 4 (y_hi: 2, y_lo: 2; y = y_hi * 2 + y_lo), z: 4, core: 2. Of those that a mesh axis runs over, the one named last changes fastest.
Arguments:
- img_feat: bfloat16 [65536, 1152], P(('dp', 'inner')), may hold values from -0.1875 to 0.1875
- txt_feat: bfloat16 [65536, 1152], P(('dp', 'inner')), may hold values from -0.1875 to 0.1875
- text_pair: int32 [65536], P(('dp', 'inner')), may hold values from 0 to 65535, as said below
- w_img: bfloat16 [1152, 1152], replicated, may hold values from -0.1875 to 0.1875
- w_txt: bfloat16 [1152, 1152], replicated, may hold values from -0.1875 to 0.1875
- logit_scale: float32 [1], replicated, may hold values from 2.3 to 3
- logit_bias: float32 [1], replicated, may hold values from -6 to -3
Outputs:
- grad_img_feat: bfloat16 [65536, 1152], P(('dp', 'inner'))
- grad_txt_feat: bfloat16 [65536, 1152], P(('dp', 'inner'))
- grad_w_img: float32 [1152, 1152], replicated
- grad_w_txt: float32 [1152, 1152], replicated
- loss_mean: float32 [1], replicated
The draws below stay inside these ranges and needn't reach their ends.
Inputs may be any that keep to these rules, and one draw needn't show every extreme that they name: `text_pair`: each text row is paired with an image row of the same block of 512 rows, and each image row with exactly one text row.
All inputs are finite; a program needn't handle non-finite values.
Results may differ from the reference program's by a relative error of at most 0.015.
Values may be sent and summed in bfloat16 or wider, within the bound.
No kernel may reach another device: no remote copies, remote signals or barrier semaphores. Data moves between devices by JAX's collectives and lax.ppermute only.
A program may use at most 128 MiB of HBM per device.

```python
import jax
import jax.numpy as jnp
import numpy as np
from jax import lax

D = 1152
TOK_DEV = 512
ROUNDS = 8
TOKENS = 65536
N_DP = 16
N_INNER = 8


def draw_text_pair(key, part):
    key = jax.random.fold_in(key, 7)
    block_count = TOKENS // TOK_DEV
    keys = jax.random.split(key, block_count)
    orders = jax.vmap(lambda one_key: jax.random.permutation(one_key, TOK_DEV))(keys)
    starts = jnp.arange(block_count, dtype=jnp.int32)[:, None] * TOK_DEV
    return (orders.astype(jnp.int32) + starts).reshape(TOKENS).astype(jnp.int32)


def level_of(own_key, extent, cuts, smallest, high):
    def one(axis_at, blocks):
        steps = jax.random.uniform(jax.random.fold_in(jax.random.fold_in(own_key, 6), axis_at), (blocks,), jnp.float32, smallest / len(cuts), high / len(cuts))
        return jnp.repeat(jnp.exp(steps), extent[axis_at] // blocks).reshape((-1,) + (1,) * (len(extent) - axis_at - 1))

    level = one(*cuts[0])
    for cut in cuts[1:]:
        level = level * one(*cut)
    return level


def noise(rng, extent, scale, most, shards=(), kind=jnp.bfloat16):
    result = scale * jax.random.normal(rng, extent, jnp.float32)
    if shards:
        result = result * level_of(rng, extent, shards, -0.22, 0.18)
    return jnp.clip(result, -most, most).astype(kind)


def setup_inputs(seed: int = 0) -> dict:
    key_of = jax.random.split(jax.random.key(seed), 8)
    img_feat = noise(key_of[0], (TOKENS, D), 0.03, 0.1875, ((0, 128),))
    txt_feat = noise(key_of[1], (TOKENS, D), 0.03, 0.1875, ((0, 128),))
    text_pair = draw_text_pair(jax.random.fold_in(key_of[7], 71), 0)
    w_img = noise(key_of[3], (D, D), D ** -0.5, 0.1875)
    w_txt = noise(key_of[4], (D, D), D ** -0.5, 0.1875)
    logit_scale = jnp.clip(jax.random.uniform(key_of[5], (1,), jnp.float32, 2.3, 3.0), 2.3, 3.0)
    logit_bias = jnp.clip(jax.random.uniform(key_of[6], (1,), jnp.float32, -6.0, -3.0), -6.0, -3.0)
    return dict(img_feat=img_feat, txt_feat=txt_feat, text_pair=text_pair, w_img=w_img, w_txt=w_txt, logit_scale=logit_scale, logit_bias=logit_bias)


def project_rows(features, weight):
    projected = jnp.dot(features, weight, preferred_element_type=jnp.float32)
    recip = jax.lax.rsqrt(lax.optimization_barrier(jnp.sum(projected * projected, axis=1, keepdims=True)) + 1e-06)
    unit = projected * recip
    return (unit.astype(jnp.bfloat16), unit, recip)

def head_backward(features, weight, unit, recip, grad_emb):
    along = lax.optimization_barrier(jnp.sum(unit * grad_emb, axis=1, keepdims=True))
    proj_grad = (recip * (grad_emb - unit * along)).astype(jnp.bfloat16)
    grad_feat = jnp.dot(proj_grad, weight.T, preferred_element_type=jnp.float32).astype(jnp.bfloat16)
    grad_weight = jnp.dot(features.T, proj_grad, preferred_element_type=jnp.float32)
    return (grad_feat, grad_weight)

def reference(img_feat, txt_feat, text_pair, w_img, w_txt, logit_scale, logit_bias):
    img_emb, img_unit, img_recip = project_rows(img_feat, w_img)
    txt_emb, txt_unit, txt_recip = project_rows(txt_feat, w_txt)
    logit_mult = jnp.exp(logit_scale[0])
    offset_value = logit_bias[0]
    img_blocks = img_emb.astype(jnp.float32).reshape(N_DP, N_INNER, TOK_DEV, D)
    txt_blocks = txt_emb.astype(jnp.float32).reshape(N_DP, N_INNER, TOK_DEV, D)
    local_pair = (text_pair % TOK_DEV).reshape(N_DP, N_INNER, 1, TOK_DEV)
    row_ids = jnp.arange(TOK_DEV, dtype=jnp.int32).reshape(1, 1, TOK_DEV, 1)
    positives = local_pair == row_ids
    loss_total = jnp.zeros((), jnp.float32)
    grad_img = jnp.zeros((N_DP, N_INNER, TOK_DEV, D), jnp.float32)
    grad_txt = jnp.zeros((N_DP, N_INNER, TOK_DEV, D), jnp.float32)
    for round_idx in range(ROUNDS):
        partner = np.arange(N_DP) ^ round_idx
        partner_txt = txt_blocks[partner]
        inner_prods = jnp.einsum('abid,abjd->abij', img_blocks, partner_txt)
        score = logit_mult * inner_prods + offset_value
        if round_idx == 0:
            label = jnp.where(positives, 1.0, -1.0).astype(jnp.float32)
        else:
            label = -jnp.ones_like(score)
        loss_total = loss_total + jnp.sum(jax.nn.softplus(-label * score))
        coefficient = (-label * jax.nn.sigmoid(-label * score) * logit_mult).astype(jnp.bfloat16).astype(jnp.float32)
        grad_img = grad_img + jnp.einsum('abij,abjd->abid', coefficient, partner_txt)
        txt_part = jnp.einsum('abij,abid->abjd', coefficient, img_blocks)
        grad_txt = grad_txt + txt_part[partner]
    grad_img = grad_img.reshape(TOKENS, D)
    grad_txt = grad_txt.reshape(TOKENS, D)
    grad_img_feat, grad_w_img = head_backward(img_feat, w_img, img_unit, img_recip, grad_img)
    grad_txt_feat, grad_w_txt = head_backward(txt_feat, w_txt, txt_unit, txt_recip, grad_txt)
    loss_mean = (loss_total / (TOKENS * ROUNDS)).reshape(1)
    return (grad_img_feat, grad_txt_feat, grad_w_img, grad_w_txt, loss_mean)
```

```python
import jax
import jax.numpy as jnp
from jax import lax
from jax.sharding import PartitionSpec as P

AXES = ("dp", "inner")
SIZES = (16, 8)
COUNT = 128
ROUNDS = 8
SEGMENTS = 4


def place_of(index):
    dp, inner = index // 8, index % 8
    return {
        "x": inner % 4,
        "y": inner // 4 * 2 + dp // 2 % 2,
        "z": dp // 4,
        "core": dp % 2,
    }


def index_of(place):
    dp = place["z"] * 4 + place["y"] % 2 * 2 + place["core"]
    return dp * 8 + place["y"] // 2 * 4 + place["x"]


def flipped(index, axis, mask):
    place = place_of(index)
    place[axis] ^= mask
    return index_of(place)


def exchange(block, partner):
    return lax.ppermute(block, AXES, [(index, partner(index)) for index in range(COUNT)])


def over_z(index):
    return flipped(index, "z", 1)


def over_y(index):
    return flipped(index, "y", 1)


def over_core(index):
    return flipped(index, "core", 1)


STEPS = (("x", 1), ("x", 3), ("y", 3), ("z", 3), ("y", 1), ("z", 1))


def step_of(core, chain, step):
    return STEPS[(core * 2 + chain + step) % len(STEPS)]


def chain_partner(chain, step):
    def partner(index):
        axis, mask = step_of(place_of(index)["core"], chain, step)
        return flipped(index, axis, mask)

    return partner


def my_bit(place, axis, mask):
    high = place[axis] >> 1
    return high if mask == 3 else (place[axis] & 1) ^ high


def own_segment(place, chain):
    by_core = []
    for core in range(2):
        first = my_bit(place, *step_of(core, chain, 0))
        second = my_bit(place, *step_of(core, chain, 1))
        by_core.append(2 * first + second)
    return jnp.where(place["core"] == 0, by_core[0], by_core[1])


def total_of_chain(part, place, chain):
    rows = part.shape[0] // SEGMENTS
    segment = own_segment(place, chain)

    def pick(block, at):
        return lax.dynamic_slice_in_dim(block, (at ^ segment) * rows, rows, 0)

    near = jnp.concatenate([pick(part, 0), pick(part, 1)], axis=0)
    away = jnp.concatenate([pick(part, 2), pick(part, 3)], axis=0)
    held = near + exchange(away, chain_partner(chain, 0))
    held = held[:rows] + exchange(held[rows:], chain_partner(chain, 1))
    for step in range(2, len(STEPS)):
        held = held + exchange(held, chain_partner(chain, step))
    held = jnp.concatenate([held, exchange(held, chain_partner(chain, 1))], axis=0)
    held = jnp.concatenate([held, exchange(held, chain_partner(chain, 0))], axis=0)
    return jnp.concatenate([pick(held, at) for at in range(SEGMENTS)], axis=0)


def total_scalar(value):
    value = value + exchange(value, over_core)
    for axis, mask in STEPS:
        value = value + exchange(value, lambda index: flipped(index, axis, mask))
    return value


def project_rows(features, weight):
    projected = jnp.dot(features, weight, preferred_element_type=jnp.float32)
    recip = lax.rsqrt(jnp.sum(projected * projected, axis=1, keepdims=True) + 1e-06)
    unit = projected * recip
    return (unit.astype(jnp.bfloat16), unit, recip)


def proj_grad_part(unit, recip, grad_emb):
    along = jnp.sum(unit * grad_emb, axis=1, keepdims=True)
    return (recip * (grad_emb - unit * along)).astype(jnp.bfloat16)


def pair_tile(image_rows, text_rows, label, logit_mult, offset_value):
    inner_prods = lax.dot_general(
        image_rows, text_rows, (((1,), (1,)), ((), ())), preferred_element_type=jnp.float32
    )
    score = logit_mult * inner_prods + offset_value
    loss_part = jnp.sum(jax.nn.softplus(-label * score))
    coefficient = (-label * jax.nn.sigmoid(-label * score) * logit_mult).astype(jnp.bfloat16)
    return (loss_part, coefficient)


def times_text(coefficient, text_rows):
    return jnp.dot(coefficient, text_rows, preferred_element_type=jnp.float32)


def times_image(coefficient, image_rows):
    return lax.dot_general(
        coefficient, image_rows, (((0,), (0,)), ((), ())), preferred_element_type=jnp.float32
    )


def weight_part(features, proj_grad):
    return lax.dot_general(
        features, proj_grad, (((0,), (0,)), ((), ())), preferred_element_type=jnp.float32
    ).astype(jnp.bfloat16)


def feature_grad(proj_grad, weight):
    return lax.dot_general(
        proj_grad, weight, (((1,), (1,)), ((), ())), preferred_element_type=jnp.float32
    ).astype(jnp.bfloat16)


def per_device(img_feat, txt_feat, text_pair, w_img, w_txt, logit_scale, logit_bias):
    row_count = img_feat.shape[0]
    dp, inner = lax.axis_index("dp"), lax.axis_index("inner")
    place = {"x": inner % 4, "y": inner // 4 * 2 + dp // 2 % 2, "z": dp // 4, "core": dp % 2}
    logit_mult = jnp.exp(logit_scale[0])
    offset_value = logit_bias[0]

    far_img_feat = exchange(img_feat, over_z)
    far_txt_feat = exchange(txt_feat, over_y)
    img_emb, img_unit, img_recip = project_rows(img_feat, w_img)
    txt_emb, txt_unit, txt_recip = project_rows(txt_feat, w_txt)
    far_img_emb, far_img_unit, far_img_recip = project_rows(far_img_feat, w_img)
    far_txt_emb, far_txt_unit, far_txt_recip = project_rows(far_txt_feat, w_txt)
    images = (img_emb, far_img_emb)
    texts = (txt_emb, exchange(txt_emb, over_core), far_txt_emb, exchange(far_txt_emb, over_core))

    positives = (text_pair % row_count)[None, :] == jnp.arange(row_count, dtype=jnp.int32)[:, None]
    own_label = jnp.where(positives, 1.0, -1.0).astype(jnp.float32)
    other_label = -jnp.ones((row_count, row_count), jnp.float32)
    loss_total = jnp.zeros((), jnp.float32)
    grad_img = [0.0, 0.0]
    grad_txt = [0.0, 0.0, 0.0, 0.0]
    for text_at, text_rows in enumerate(texts):
        for image_at, image_rows in enumerate(images):
            label = own_label if text_at == 0 and image_at == 0 else other_label
            loss_part, coefficient = pair_tile(
                image_rows, text_rows, label, logit_mult, offset_value
            )
            loss_total = loss_total + loss_part
            grad_img[image_at] += times_text(coefficient, text_rows)
            grad_txt[text_at] += times_image(coefficient, image_rows)
    own_txt_grad = grad_txt[0] + exchange(grad_txt[1].astype(jnp.bfloat16), over_core)
    far_txt_grad = grad_txt[2] + exchange(grad_txt[3].astype(jnp.bfloat16), over_core)

    img_pg = proj_grad_part(img_unit, img_recip, grad_img[0])
    far_img_pg = proj_grad_part(far_img_unit, far_img_recip, grad_img[1])
    txt_pg = proj_grad_part(txt_unit, txt_recip, own_txt_grad)
    far_txt_pg = proj_grad_part(far_txt_unit, far_txt_recip, far_txt_grad)
    full_img_pg = img_pg + exchange(far_img_pg, over_z)
    full_txt_pg = txt_pg + exchange(far_txt_pg, over_y)
    grad_img_feat = feature_grad(full_img_pg, w_img)
    grad_txt_feat = feature_grad(full_txt_pg, w_txt)

    img_part = weight_part(
        jnp.concatenate([img_feat, far_img_feat]), jnp.concatenate([img_pg, far_img_pg])
    )
    txt_part = weight_part(
        jnp.concatenate([txt_feat, far_txt_feat]), jnp.concatenate([txt_pg, far_txt_pg])
    )
    first_core = place["core"] == 0
    own_part = jnp.where(first_core, img_part, txt_part)
    their_part = jnp.where(first_core, txt_part, img_part)
    own_part = own_part + exchange(their_part, over_core)
    half = own_part.shape[0] // 2
    totals = [total_of_chain(own_part[at * half : (at + 1) * half], place, at) for at in range(2)]
    own_total = jnp.concatenate(totals)
    their_total = exchange(own_total, over_core)
    grad_w_img = jnp.where(first_core, own_total, their_total).astype(jnp.float32)
    grad_w_txt = jnp.where(first_core, their_total, own_total).astype(jnp.float32)
    loss_sum = total_scalar(loss_total.reshape(1, 1))
    loss_mean = (loss_sum / (row_count * COUNT * ROUNDS)).reshape(1)
    return (grad_img_feat, grad_txt_feat, grad_w_img, grad_w_txt, loss_mean)


def solution(mesh):
    return jax.shard_map(
        per_device,
        mesh=mesh,
        in_specs=(
            P(("dp", "inner"), None),
            P(("dp", "inner"), None),
            P(("dp", "inner")),
            P(),
            P(),
            P(),
            P(),
        ),
        out_specs=(P(("dp", "inner"), None), P(("dp", "inner"), None), P(), P(), P()),
        check_vma=False,
    )
```

```python
import jax
import jax.numpy as jnp
from jax import lax
from jax.experimental import pallas as pl
from jax.experimental.pallas import tpu as pltpu
from jax.sharding import PartitionSpec as P

AXES = ("dp", "inner")
COUNT = 128
CHIPS = 64
ROUNDS = 8
ROWS, WIDTH, LANES = 512, 1152, 128
SEGS, SEG_ROWS, SLAB = 4, 144, 16
VMEM_LIMIT = 56 * 1024 * 1024
LOG2E = 1.4426950408889634
bf16, f32 = jnp.bfloat16, jnp.float32
VM = pl.BlockSpec(memory_space=pltpu.VMEM)
SM = pl.BlockSpec(memory_space=pltpu.SMEM)
HBM = pl.BlockSpec(memory_space=pl.ANY)
TALL = jax.ShapeDtypeStruct((2, ROWS, WIDTH), bf16)
FLAT = jax.ShapeDtypeStruct((ROWS, WIDTH), bf16)
WIDE = jax.ShapeDtypeStruct((ROWS, WIDTH), f32)
LOSS = jax.ShapeDtypeStruct((1, ROWS), f32)
RECIP = jax.ShapeDtypeStruct((ROWS, LANES), f32)
PIECES = jax.ShapeDtypeStruct((SEGS, SEG_ROWS, WIDTH), bf16)


def place_of(index):
    dp, inner = index // 8, index % 8
    return {
        "x": inner % 4,
        "y": inner // 4 * 2 + dp // 2 % 2,
        "z": dp // 4,
        "core": dp % 2,
    }


def index_of(place):
    dp = place["z"] * 4 + place["y"] % 2 * 2 + place["core"]
    return dp * 8 + place["y"] // 2 * 4 + place["x"]


def flipped(index, axis, mask):
    place = place_of(index)
    place[axis] ^= mask
    return index_of(place)


def exchange(block, partner):
    return lax.ppermute(block, AXES, [(index, partner(index)) for index in range(COUNT)])


def over_z(index):
    return flipped(index, "z", 1)


def over_y(index):
    return flipped(index, "y", 1)


def over_core(index):
    return flipped(index, "core", 1)


STEPS = (("x", 1), ("x", 3), ("y", 3), ("z", 3), ("y", 1), ("z", 1))


STEPS = (("x", 1), ("x", 3), ("y", 3), ("z", 3), ("y", 1), ("z", 1))


def step_of(core, chain, step):
    return STEPS[(core * 2 + chain + step) % len(STEPS)]


def chain_partner(chain, step):
    def partner(index):
        axis, mask = step_of(place_of(index)["core"], chain, step)
        return flipped(index, axis, mask)

    return partner


def my_bit(place, axis, mask):
    high = place[axis] >> 1
    return high if mask == 3 else (place[axis] & 1) ^ high


def segment_of(place, core, chain):
    first = my_bit(place, *step_of(core, chain, 0))
    second = my_bit(place, *step_of(core, chain, 1))
    return 2 * first + second


def piece_order(place, chain):
    order = []
    for core in range(2):
        order += [at ^ segment_of(place, core, chain) for at in range(SEGS)]
    order += [(place["core"] == core).astype(jnp.int32) for core in range(2)]
    return jnp.stack(order).astype(jnp.int32)


def total_start(keep, send, chain, slab):
    pieces = (keep + exchange(send, over_core)).reshape(SEGS * SEG_ROWS, WIDTH)
    half = SEGS * SEG_ROWS // 2
    held = jnp.concatenate([pieces[:half], slab])
    held = held + exchange(jnp.concatenate([pieces[half:], slab]), chain_partner(chain, 0))
    tail = held[half:]
    away = jnp.concatenate([held[SEG_ROWS:half], tail])
    return jnp.concatenate([held[:SEG_ROWS], tail]) + exchange(away, chain_partner(chain, 1))


def total_end(held, chain):
    held = held[:SEG_ROWS]
    held = jnp.concatenate([held, exchange(held, chain_partner(chain, 1))])
    held = jnp.concatenate([held, exchange(held, chain_partner(chain, 0))])
    return held.reshape(SEGS, SEG_ROWS, WIDTH)


def loss_slab(loss, chip):
    high = lax.reduce_precision(loss, 8, 7)
    rest = loss - high
    middle = lax.reduce_precision(rest, 8, 7)
    low = rest - middle
    lane = lax.broadcasted_iota(jnp.int32, (SLAB, WIDTH), 1)
    row = lax.broadcasted_iota(jnp.int32, (SLAB, WIDTH), 0)
    at = jnp.where(row == 0, lane - 3 * chip, -1)
    slab = jnp.where(at == 0, high, jnp.where(at == 1, middle, jnp.where(at == 2, low, 0.0)))
    return slab.astype(bf16)


def cost(flops):
    return pl.CostEstimate(flops=flops, bytes_accessed=8_000_000, transcendentals=0)


def project_kernel(feat_ref, weight_ref, emb_ref, recip_ref):
    projected = jnp.dot(feat_ref[...], weight_ref[...], preferred_element_type=f32)
    recip = lax.rsqrt(jnp.sum(projected * projected, axis=1, keepdims=True) + 1e-06)
    emb_ref[...] = (projected * recip).astype(bf16)
    recip_ref[...] = jnp.broadcast_to(recip, recip_ref.shape)


def project(features, weight, limit=16):
    return pl.pallas_call(
        project_kernel,
        in_specs=[VM, VM],
        out_specs=[VM, VM],
        out_shape=[FLAT, RECIP],
        compiler_params=pltpu.CompilerParams(vmem_limit_bytes=limit << 20),
        cost_estimate=cost(2 * ROWS * WIDTH * WIDTH),
    )(features, weight)


def pair_job(image, text, scale_ref, positive):
    score = lax.dot_general(image, text, (((1,), (1,)), ((), ())), preferred_element_type=f32)
    score = score * scale_ref[0] + scale_ref[1]
    if positive is not None:
        score = jnp.where(positive, -score, score)
    power = jnp.exp2(score)
    whole = power + 1.0
    coefficient = (power * scale_ref[2]) * pl.reciprocal(whole, approx=True)
    if positive is not None:
        coefficient = jnp.where(positive, -coefficient, coefficient)
    quarter = whole.shape[0] // 4
    product = (whole[:quarter] * whole[quarter : 2 * quarter]) * (
        whole[2 * quarter : 3 * quarter] * whole[3 * quarter :]
    )
    loss = jnp.sum(jnp.log(product), axis=0, keepdims=True)
    return loss, coefficient.astype(bf16)


def times_text(coefficient, text):
    return jnp.dot(coefficient, text, preferred_element_type=f32)


def times_image(coefficient, image):
    return lax.dot_general(
        coefficient, image, (((0,), (0,)), ((), ())), preferred_element_type=f32
    )


def proj_grad(emb, recip, grad):
    emb = emb.astype(f32)
    along = jnp.sum(emb * grad, axis=1, keepdims=True)
    return (recip[:, :1] * (grad - emb * along)).astype(bf16)


def near_kernel(scale_ref, pair_ref, img_ref, txt_ref, other_ref, gi_ref, gt_ref, go_ref, loss_ref):
    rows = img_ref.shape[0]
    positive = pair_ref[...] == lax.broadcasted_iota(jnp.int32, (rows, rows), 0)
    loss, coefficient = pair_job(img_ref[...], txt_ref[...], scale_ref, positive)
    gt_ref[...] = times_image(coefficient, img_ref[...])
    gi_ref[...] = times_text(coefficient, txt_ref[...])
    more, coefficient = pair_job(img_ref[...], other_ref[...], scale_ref, None)
    go_ref[...] = times_image(coefficient, img_ref[...])
    gi_ref[...] += times_text(coefficient, other_ref[...])
    loss_ref[...] = loss + more


def near_pairs(scale, pair, img, txt, other):
    return pl.pallas_call(
        near_kernel,
        in_specs=[SM] + [VM] * 4,
        out_specs=[VM] * 4,
        out_shape=[WIDE, WIDE, WIDE, LOSS],
        compiler_params=pltpu.CompilerParams(vmem_limit_bytes=VMEM_LIMIT),
        cost_estimate=cost(12 * ROWS * ROWS * WIDTH),
    )(scale, pair, img, txt, other)


def far_kernel(
    scale_ref, img_in, far_in, txt_in, other_in, far_txt_in, far_other_in, recip_in, far_recip_in,
    gi_in, gt_in, go_in,
    pg_out, gt_out, gft_out, send_out, loss_ref,
    img, far, txt, other, far_txt, far_other, recip, far_recip,
    gi, gf, gt, go, gft, pg, send, sems, out_sems,
):
    def copy_in(at, source, target):
        copy = pltpu.make_async_copy(source, target, sems.at[at])
        copy.start()
        return copy

    def copy_out(at, source, target):
        copy = pltpu.make_async_copy(source, target, out_sems.at[at])
        copy.start()
        return copy

    c_far = copy_in(0, far_in, far)
    c_other = copy_in(1, other_in, other)
    c_img = copy_in(2, img_in, img)
    c_far_other = copy_in(3, far_other_in, far_other)
    c_go = copy_in(4, go_in, go)
    c_gi = copy_in(5, gi_in, gi)
    c_txt = copy_in(6, txt_in, txt)
    c_gt = copy_in(7, gt_in, gt)
    c_far_txt = copy_in(8, far_txt_in, far_txt)
    c_recip = copy_in(9, recip_in, recip)
    c_far_recip = copy_in(10, far_recip_in, far_recip)

    c_far.wait()
    c_other.wait()
    loss, last = pair_job(far[...], other[...], scale_ref, None)
    c_img.wait()
    c_far_other.wait()
    more, first = pair_job(img[...], far_other[...], scale_ref, None)
    loss += more
    c_go.wait()
    send[0] = (go[...] + times_image(last, far[...])).astype(bf16)
    out_0 = copy_out(0, send.at[0], send_out.at[0])
    gf[...] = times_text(last, other[...])
    more, second = pair_job(far[...], far_other[...], scale_ref, None)
    loss += more
    c_gi.wait()
    gi[...] += times_text(first, far_other[...])
    send[1] = (times_image(first, img[...]) + times_image(second, far[...])).astype(bf16)
    out_1 = copy_out(1, send.at[1], send_out.at[1])
    c_txt.wait()
    more, last = pair_job(far[...], txt[...], scale_ref, None)
    loss += more
    gf[...] += times_text(second, far_other[...])
    c_far_txt.wait()
    more, first = pair_job(img[...], far_txt[...], scale_ref, None)
    loss += more
    c_gt.wait()
    gt[...] += times_image(last, far[...])
    out_2 = copy_out(2, gt, gt_out)
    gf[...] += times_text(last, txt[...])
    more, second = pair_job(far[...], far_txt[...], scale_ref, None)
    loss += more
    loss_ref[...] = loss
    c_recip.wait()
    c_far_recip.wait()
    gi[...] += times_text(first, far_txt[...])
    pg[0] = proj_grad(img[...], recip[...], gi[...])
    out_4 = copy_out(4, pg.at[0], pg_out.at[0])
    gf[...] += times_text(second, far_txt[...])
    pg[1] = proj_grad(far[...], far_recip[...], gf[...])
    out_5 = copy_out(5, pg.at[1], pg_out.at[1])
    gft[...] = times_image(first, img[...]) + times_image(second, far[...])
    out_3 = copy_out(3, gft, gft_out)
    for copy in (out_0, out_1, out_2, out_4, out_5, out_3):
        copy.wait()


def far_pairs(*operands):
    flat, wide = pltpu.VMEM((ROWS, WIDTH), bf16), pltpu.VMEM((ROWS, WIDTH), f32)
    line, tall = pltpu.VMEM((ROWS, LANES), f32), pltpu.VMEM((2, ROWS, WIDTH), bf16)
    return pl.pallas_call(
        far_kernel,
        in_specs=[SM] + [HBM] * 11,
        out_specs=[HBM] * 4 + [VM],
        out_shape=[TALL, WIDE, WIDE, TALL, LOSS],
        scratch_shapes=[flat] * 6 + [line] * 2 + [wide] * 5 + [tall] * 2
        + [pltpu.SemaphoreType.DMA((11,)), pltpu.SemaphoreType.DMA((6,))],
        compiler_params=pltpu.CompilerParams(vmem_limit_bytes=VMEM_LIMIT),
        cost_estimate=cost(36 * ROWS * ROWS * WIDTH),
    )(*operands)


def head_part(order_ref, feat, pg, stage, keep_out, send_out, sems):
    third = WIDTH // 3
    pending = []
    done = 0
    for at in range(3):
        columns = feat[:, at * third : (at + 1) * third]
        part = lax.dot_general(columns, pg, (((0,), (0,)), ((), ())), preferred_element_type=f32)
        stage[at * third : (at + 1) * third] = part.astype(bf16)
        while (done + 1) * SEG_ROWS <= (at + 1) * third:
            here = stage.at[pl.ds(done * SEG_ROWS, SEG_ROWS)]
            mine, to = order_ref[2 * SEGS + done // SEGS], order_ref[done]
            keep = pltpu.make_async_copy(here, keep_out.at[to], sems.at[done])
            send = pltpu.make_async_copy(here, send_out.at[to], sems.at[done])
            pl.when(mine == 1)(keep.start)
            pl.when(mine == 0)(send.start)
            pending.append(keep)
            done += 1
    for copy in pending:
        copy.wait()


def image_head_kernel(order_ref, feat_in, far_in, pg_in, keep_out, send_out, feat, pg, stage, sems, out_sems):
    copies = [
        pltpu.make_async_copy(pg_in.at[0], pg.at[pl.ds(0, ROWS)], sems.at[0]),
        pltpu.make_async_copy(feat_in, feat.at[pl.ds(0, ROWS)], sems.at[1]),
        pltpu.make_async_copy(pg_in.at[1], pg.at[pl.ds(ROWS, ROWS)], sems.at[2]),
        pltpu.make_async_copy(far_in, feat.at[pl.ds(ROWS, ROWS)], sems.at[3]),
    ]
    for copy in copies:
        copy.start()
    for copy in copies:
        copy.wait()
    head_part(order_ref, feat, pg[...], stage, keep_out, send_out, out_sems)


def image_head(order, feat, far, pg):
    both = pltpu.VMEM((2 * ROWS, WIDTH), bf16)
    return pl.pallas_call(
        image_head_kernel,
        in_specs=[SM] + [HBM] * 3,
        out_specs=[HBM] * 2,
        out_shape=[PIECES, PIECES],
        scratch_shapes=[both, both, pltpu.VMEM((WIDTH, WIDTH), bf16)]
        + [pltpu.SemaphoreType.DMA((4,)), pltpu.SemaphoreType.DMA((2 * SEGS,))],
        compiler_params=pltpu.CompilerParams(vmem_limit_bytes=VMEM_LIMIT),
        cost_estimate=cost(4 * ROWS * WIDTH * WIDTH),
    )(order, feat, far, pg)


def text_head_kernel(
    order_ref, feat_in, far_in, emb_in, far_emb_in, recip_in, far_recip_in, gt_in, gft_in, got_in,
    pg_out, keep_out, send_out,
    feat, emb, recip, grad, got, pg, stage, sems, out_sems, pg_sems,
):
    low, high = pl.ds(0, ROWS), pl.ds(ROWS, ROWS)
    pairs = [
        (gt_in, grad.at[0]), (emb_in, emb.at[0]), (got_in.at[0], got.at[0]), (recip_in, recip.at[0]),
        (gft_in, grad.at[1]), (far_emb_in, emb.at[1]), (got_in.at[1], got.at[1]), (far_recip_in, recip.at[1]),
        (feat_in, feat.at[low]), (far_in, feat.at[high]),
    ]
    copies = [
        pltpu.make_async_copy(source, target, sems.at[at]) for at, (source, target) in enumerate(pairs)
    ]
    for copy in copies:
        copy.start()
    outs = []
    for at, rows in enumerate((low, high)):
        for copy in copies[4 * at : 4 * at + 4]:
            copy.wait()
        pg[rows] = proj_grad(emb[at], recip[at], grad[at] + got[at].astype(f32))
        out = pltpu.make_async_copy(pg.at[rows], pg_out.at[at], pg_sems.at[at])
        out.start()
        outs.append(out)
    for copy in copies[8:]:
        copy.wait()
    head_part(order_ref, feat, pg[...], stage, keep_out, send_out, out_sems)
    for out in outs:
        out.wait()


def text_head(*operands):
    both, tall = pltpu.VMEM((2 * ROWS, WIDTH), bf16), pltpu.VMEM((2, ROWS, WIDTH), bf16)
    return pl.pallas_call(
        text_head_kernel,
        in_specs=[SM] + [HBM] * 9,
        out_specs=[HBM] * 3,
        out_shape=[TALL, PIECES, PIECES],
        scratch_shapes=[both, tall, pltpu.VMEM((2, ROWS, LANES), f32), pltpu.VMEM((2, ROWS, WIDTH), f32),
            tall, both, pltpu.VMEM((WIDTH, WIDTH), bf16)]
        + [pltpu.SemaphoreType.DMA((10,)), pltpu.SemaphoreType.DMA((2 * SEGS,)), pltpu.SemaphoreType.DMA((2,))],
        compiler_params=pltpu.CompilerParams(vmem_limit_bytes=VMEM_LIMIT),
        cost_estimate=cost(4 * ROWS * WIDTH * WIDTH),
    )(*operands)


def widen_kernel(order_ref, own_ref, their_ref, total_ref):
    at = pl.program_id(0)
    mine = order_ref[2 * SEGS + at // SEGS] == 1
    position = order_ref[at]

    @pl.when(mine)
    def _():
        total_ref[...] = own_ref[position].astype(f32)

    @pl.when(jnp.logical_not(mine))
    def _():
        total_ref[...] = their_ref[position].astype(f32)


def widen(order, own, their):
    whole = pl.BlockSpec((SEGS, SEG_ROWS, WIDTH), lambda at: (0, 0, 0))
    return pl.pallas_call(
        widen_kernel,
        grid=(2 * SEGS,),
        in_specs=[SM, whole, whole],
        out_specs=pl.BlockSpec((SEG_ROWS, WIDTH), lambda at: (at, 0)),
        out_shape=jax.ShapeDtypeStruct((WIDTH, WIDTH), f32),
        compiler_params=pltpu.CompilerParams(vmem_limit_bytes=VMEM_LIMIT),
        cost_estimate=cost(1_000_000),
    )(order, own, their)


def feature_grad(part, got, weight):
    total = (part.astype(f32) + got.astype(f32)).astype(bf16)
    return lax.dot_general(
        total, weight, (((1,), (1,)), ((), ())), preferred_element_type=f32
    ).astype(bf16)


def per_device(img_feat, txt_feat, text_pair, w_img, w_txt, logit_scale, logit_bias):
    dp, inner = lax.axis_index("dp"), lax.axis_index("inner")
    place = {"x": inner % 4, "y": inner // 4 * 2 + dp // 2 % 2, "z": dp // 4, "core": dp % 2}
    chip = (place["z"] * 4 + place["y"]) * 4 + place["x"]
    orders = [piece_order(place, chain) for chain in range(2)]
    mult = jnp.exp(logit_scale[0])
    scale = jnp.stack([mult * LOG2E, logit_bias[0] * LOG2E, mult])
    pair = (text_pair % ROWS)[None, :]

    far_txt_feat = exchange(txt_feat, over_y)
    far_img_feat = exchange(img_feat, over_z)
    txt_emb, txt_recip = project(txt_feat, w_txt)
    other_emb = exchange(txt_emb, over_core)
    img_emb, img_recip = project(img_feat, w_img)
    grad_img, grad_txt, grad_other, near_loss = near_pairs(scale, pair, img_emb, txt_emb, other_emb)

    far_txt_emb, far_txt_recip = project(far_txt_feat, w_txt)
    far_other_emb = exchange(far_txt_emb, over_core)
    far_img_emb, far_img_recip = project(far_img_feat, w_img)
    img_pg, grad_txt, grad_far_txt, grad_other, far_loss = far_pairs(
        scale, img_emb, far_img_emb, txt_emb, other_emb, far_txt_emb, far_other_emb,
        img_recip, far_img_recip, grad_img, grad_txt, grad_other,
    )
    got_grad = exchange(grad_other, over_core)
    loss = jnp.sum(near_loss + far_loss)
    loss = loss + exchange(loss.reshape(1, 1), over_core)[0, 0]
    img_got = exchange(img_pg[1], over_z)
    img_keep, img_send = image_head(orders[0], img_feat, far_img_feat, img_pg)
    txt_pg, txt_keep, txt_send = text_head(
        orders[1], txt_feat, far_txt_feat, txt_emb, far_txt_emb,
        txt_recip, far_txt_recip, grad_txt, grad_far_txt, got_grad,
    )
    txt_got = exchange(txt_pg[1], over_y)

    slabs = (loss_slab(loss, chip), jnp.zeros((0, WIDTH), bf16))
    img_held = total_start(img_keep, img_send, 0, slabs[0])
    txt_held = total_start(txt_keep, txt_send, 1, slabs[1])
    for step in range(2, len(STEPS)):
        img_more = exchange(img_held, chain_partner(0, step))
        txt_more = exchange(txt_held, chain_partner(1, step))
        if step == 4:
            grad_img_feat = feature_grad(img_pg[0], img_got, w_img)
            img_more, grad_img_feat = lax.optimization_barrier((img_more, grad_img_feat))
        if step == 5:
            grad_txt_feat = feature_grad(txt_pg[0], txt_got, w_txt)
            txt_more, grad_txt_feat = lax.optimization_barrier((txt_more, grad_txt_feat))
        img_held = img_held + img_more
        txt_held = txt_held + txt_more
    loss_mean = (jnp.sum(img_held[SEG_ROWS:].astype(f32)) / (ROWS * COUNT * ROUNDS)).reshape(1)
    img_total = total_end(img_held, 0)
    txt_total = total_end(txt_held, 1)
    grad_w_img = widen(orders[0], img_total, exchange(img_total, over_core))
    grad_w_txt = widen(orders[1], txt_total, exchange(txt_total, over_core))
    return (grad_img_feat, grad_txt_feat, grad_w_img, grad_w_txt, loss_mean)


def solution(mesh):
    return jax.shard_map(
        per_device,
        mesh=mesh,
        in_specs=(
            P(("dp", "inner"), None),
            P(("dp", "inner"), None),
            P(("dp", "inner")),
            P(),
            P(),
            P(),
            P(),
        ),
        out_specs=(P(("dp", "inner"), None), P(("dp", "inner"), None), P(), P(), P()),
        check_vma=False,
    )
```

```python
import jax
import jax.numpy as jnp
from jax import lax
from jax.experimental import pallas as pl
from jax.experimental.pallas import tpu as pltpu
from jax.sharding import PartitionSpec as P

AXES = ("dp", "inner")
COUNT = 128
ROUNDS = 8
ROWS, WIDTH, LANES = 512, 1152, 128
SEGS, SEG_ROWS, SLAB = 4, 144, 16
MIB = 1024 * 1024
LOG2E = 1.4426950408889634
bf16, f32 = jnp.bfloat16, jnp.float32
VM = pl.BlockSpec(memory_space=pltpu.VMEM)
SM = pl.BlockSpec(memory_space=pltpu.SMEM)
HBM = pl.BlockSpec(memory_space=pl.ANY)
TALL = jax.ShapeDtypeStruct((2, ROWS, WIDTH), bf16)
FLAT = jax.ShapeDtypeStruct((ROWS, WIDTH), bf16)
WIDE = jax.ShapeDtypeStruct((ROWS, WIDTH), f32)
LOSS = jax.ShapeDtypeStruct((1, ROWS), f32)
RECIP = jax.ShapeDtypeStruct((ROWS, LANES), f32)
SLAB_SHAPE = jax.ShapeDtypeStruct((SLAB, WIDTH), bf16)
IMG_PIECES = jax.ShapeDtypeStruct((SEGS, SEG_ROWS + SLAB, WIDTH), bf16)
TXT_PIECES = jax.ShapeDtypeStruct((SEGS, SEG_ROWS, WIDTH), bf16)


def place_of(index):
    dp, inner = index // 8, index % 8
    return {
        "x": inner % 4,
        "y": inner // 4 * 2 + dp // 2 % 2,
        "z": dp // 4,
        "core": dp % 2,
    }


def index_of(place):
    dp = place["z"] * 4 + place["y"] % 2 * 2 + place["core"]
    return dp * 8 + place["y"] // 2 * 4 + place["x"]


def flipped(index, axis, mask):
    place = place_of(index)
    place[axis] ^= mask
    return index_of(place)


def exchange(block, partner):
    return lax.ppermute(block, AXES, [(index, partner(index)) for index in range(COUNT)])


def over_z(index):
    return flipped(index, "z", 1)


def over_y(index):
    return flipped(index, "y", 1)


def over_core(index):
    return flipped(index, "core", 1)


STEPS = (("x", 1), ("x", 3), ("y", 3), ("z", 3), ("y", 1), ("z", 1))


STEPS = (("x", 1), ("x", 3), ("y", 3), ("z", 3), ("y", 1), ("z", 1))


def step_of(core, chain, step):
    return STEPS[(core * 2 + chain + step) % len(STEPS)]


def chain_partner(chain, step):
    def partner(index):
        axis, mask = step_of(place_of(index)["core"], chain, step)
        return flipped(index, axis, mask)

    return partner


def my_bit(place, axis, mask):
    high = place[axis] >> 1
    return high if mask == 3 else (place[axis] & 1) ^ high


def segment_of(place, core, chain):
    first = my_bit(place, *step_of(core, chain, 0))
    second = my_bit(place, *step_of(core, chain, 1))
    return 2 * first + second


def piece_order(place, chain):
    order = []
    for core in range(2):
        order += [at ^ segment_of(place, core, chain) for at in range(SEGS)]
    order += [(place["core"] == core).astype(jnp.int32) for core in range(2)]
    return jnp.stack(order).astype(jnp.int32)


def over_chain(blocks, step, extra=()):
    got = [exchange(block, chain_partner(chain, step)) for chain, block in enumerate(blocks)]
    out = lax.optimization_barrier((*got, *extra))
    return out[: len(blocks)], out[len(blocks) :]


def cost(flops):
    return pl.CostEstimate(flops=1, bytes_accessed=1, transcendentals=0)


def project_kernel(feat_ref, weight_ref, emb_ref, recip_ref):
    projected = jnp.dot(feat_ref[...], weight_ref[...], preferred_element_type=f32)
    recip = lax.rsqrt(jnp.sum(projected * projected, axis=1, keepdims=True) + 1e-06)
    emb_ref[...] = (projected * recip).astype(bf16)
    recip_ref[...] = jnp.broadcast_to(recip, recip_ref.shape)


def project(features, weight, limit=16):
    return pl.pallas_call(
        project_kernel,
        in_specs=[VM, VM],
        out_specs=[VM, VM],
        out_shape=[FLAT, RECIP],
        compiler_params=pltpu.CompilerParams(vmem_limit_bytes=limit << 20),
        cost_estimate=cost(2 * ROWS * WIDTH * WIDTH),
    )(features, weight)


def pair_job(image, text, scale_ref, positive):
    score = lax.dot_general(image, text, (((1,), (1,)), ((), ())), preferred_element_type=f32)
    score = score * scale_ref[0] + scale_ref[1]
    if positive is not None:
        score = jnp.where(positive, -score, score)
    power = jnp.exp2(score)
    whole = power + 1.0
    coefficient = (power * scale_ref[2]) * pl.reciprocal(whole, approx=True)
    if positive is not None:
        coefficient = jnp.where(positive, -coefficient, coefficient)
    quarter = whole.shape[0] // 4
    product = (whole[:quarter] * whole[quarter : 2 * quarter]) * (
        whole[2 * quarter : 3 * quarter] * whole[3 * quarter :]
    )
    loss = jnp.sum(jnp.log(product), axis=0, keepdims=True)
    return loss, coefficient.astype(bf16)


def times_text(coefficient, text):
    return jnp.dot(coefficient, text, preferred_element_type=f32)


def times_image(coefficient, image):
    return lax.dot_general(
        coefficient, image, (((0,), (0,)), ((), ())), preferred_element_type=f32
    )


def proj_grad(emb, recip, grad):
    emb = emb.astype(f32)
    along = jnp.sum(emb * grad, axis=1, keepdims=True)
    return (recip[:, :1] * (grad - emb * along)).astype(bf16)


def near_kernel(scale_ref, pair_ref, img_ref, txt_ref, other_ref, gi_ref, gt_ref, go_ref, loss_ref):
    rows = img_ref.shape[0]
    positive = pair_ref[...] == lax.broadcasted_iota(jnp.int32, (rows, rows), 0)
    loss, coefficient = pair_job(img_ref[...], txt_ref[...], scale_ref, positive)
    gt_ref[...] = times_image(coefficient, img_ref[...])
    gi_ref[...] = times_text(coefficient, txt_ref[...])
    more, coefficient = pair_job(img_ref[...], other_ref[...], scale_ref, None)
    go_ref[...] = times_image(coefficient, img_ref[...])
    gi_ref[...] += times_text(coefficient, other_ref[...])
    loss_ref[...] = loss + more


def near_pairs(scale, pair, img, txt, other):
    return pl.pallas_call(
        near_kernel,
        in_specs=[SM] + [VM] * 4,
        out_specs=[VM] * 4,
        out_shape=[WIDE, WIDE, WIDE, LOSS],
        compiler_params=pltpu.CompilerParams(vmem_limit_bytes=24 * MIB),
        cost_estimate=cost(12 * ROWS * ROWS * WIDTH),
    )(scale, pair, img, txt, other)


def far_kernel(
    scale_ref, img_in, far_in, txt_in, other_in, far_txt_in, far_other_in, recip_in, far_recip_in,
    gi_in, gt_in, go_in, near_loss_ref, chip_ref,
    pg_out, far_pg_out, gt_out, gft_out, send_out, slab_ref,
    img, far, txt, other, far_txt, far_other, recip, far_recip,
    gi, gf, gt, go, gft, pg, send, sems, out_sems,
):
    def copy_in(at, source, target):
        copy = pltpu.make_async_copy(source, target, sems.at[at])
        copy.start()
        return copy

    def copy_out(at, source, target):
        copy = pltpu.make_async_copy(source, target, out_sems.at[at])
        copy.start()
        return copy

    c_far = copy_in(0, far_in, far)
    c_other = copy_in(1, other_in, other)
    c_img = copy_in(2, img_in, img)
    c_far_other = copy_in(3, far_other_in, far_other)
    c_go = copy_in(4, go_in, go)
    c_gi = copy_in(5, gi_in, gi)
    c_txt = copy_in(6, txt_in, txt)
    c_gt = copy_in(7, gt_in, gt)
    c_far_txt = copy_in(8, far_txt_in, far_txt)
    c_recip = copy_in(9, recip_in, recip)
    c_far_recip = copy_in(10, far_recip_in, far_recip)

    c_far.wait()
    c_other.wait()
    loss, last = pair_job(far[...], other[...], scale_ref, None)
    c_img.wait()
    c_far_other.wait()
    more, first = pair_job(img[...], far_other[...], scale_ref, None)
    loss += more
    c_go.wait()
    send[0] = (go[...] + times_image(last, far[...])).astype(bf16)
    out_0 = copy_out(0, send.at[0], send_out.at[0])
    gf[...] = times_text(last, other[...])
    more, second = pair_job(far[...], far_other[...], scale_ref, None)
    loss += more
    c_gi.wait()
    gi[...] += times_text(first, far_other[...])
    send[1] = (times_image(first, img[...]) + times_image(second, far[...])).astype(bf16)
    out_1 = copy_out(1, send.at[1], send_out.at[1])
    c_txt.wait()
    more, last = pair_job(far[...], txt[...], scale_ref, None)
    loss += more
    gf[...] += times_text(second, far_other[...])
    c_far_txt.wait()
    more, first = pair_job(img[...], far_txt[...], scale_ref, None)
    loss += more
    c_gt.wait()
    gt[...] += times_image(last, far[...])
    out_2 = copy_out(2, gt, gt_out)
    gf[...] += times_text(last, txt[...])
    more, second = pair_job(far[...], far_txt[...], scale_ref, None)
    loss += more
    slab_ref[...] = loss_slab(loss + near_loss_ref[...], chip_ref[0])
    c_recip.wait()
    c_far_recip.wait()
    gi[...] += times_text(first, far_txt[...])
    pg[0] = proj_grad(img[...], recip[...], gi[...])
    out_4 = copy_out(4, pg.at[0], pg_out)
    gf[...] += times_text(second, far_txt[...])
    pg[1] = proj_grad(far[...], far_recip[...], gf[...])
    out_5 = copy_out(5, pg.at[1], far_pg_out)
    gft[...] = times_image(first, img[...]) + times_image(second, far[...])
    out_3 = copy_out(3, gft, gft_out)
    for copy in (out_0, out_1, out_2, out_4, out_5, out_3):
        copy.wait()


def loss_slab(loss, slot):
    loss = jnp.sum(loss, axis=1, keepdims=True)
    high = loss.astype(bf16).astype(f32)
    rest = loss - high
    middle = rest.astype(bf16).astype(f32)
    low = rest - middle
    lane = lax.broadcasted_iota(jnp.int32, (SLAB, WIDTH), 1)
    row = lax.broadcasted_iota(jnp.int32, (SLAB, WIDTH), 0)
    at = jnp.where(row == 0, lane - 3 * slot, -1)
    slab = jnp.where(at == 0, high, jnp.where(at == 1, middle, jnp.where(at == 2, low, 0.0)))
    return slab.astype(bf16)


def far_pairs(*operands):
    flat, wide = pltpu.VMEM((ROWS, WIDTH), bf16), pltpu.VMEM((ROWS, WIDTH), f32)
    line, tall = pltpu.VMEM((ROWS, LANES), f32), pltpu.VMEM((2, ROWS, WIDTH), bf16)
    return pl.pallas_call(
        far_kernel,
        in_specs=[SM] + [HBM] * 11 + [VM, SM],
        out_specs=[HBM] * 5 + [VM],
        out_shape=[FLAT, FLAT, WIDE, WIDE, TALL, SLAB_SHAPE],
        scratch_shapes=[flat] * 6 + [line] * 2 + [wide] * 5 + [tall] * 2
        + [pltpu.SemaphoreType.DMA((11,)), pltpu.SemaphoreType.DMA((6,))],
        compiler_params=pltpu.CompilerParams(vmem_limit_bytes=40 * MIB),
        cost_estimate=cost(36 * ROWS * ROWS * WIDTH),
    )(*operands)


def head_part(order_ref, feat, pg, stage, keep_out, send_out, sems):
    third = WIDTH // 3
    pitch = keep_out.shape[1]
    pending = []
    done = 0
    for at in range(3):
        columns = feat[:, at * third : (at + 1) * third]
        part = lax.dot_general(columns, pg, (((0,), (0,)), ((), ())), preferred_element_type=f32)
        part = part.astype(bf16)
        for piece in range(2 * SEGS):
            low = max(piece * SEG_ROWS, at * third)
            high = min((piece + 1) * SEG_ROWS, (at + 1) * third)
            if low < high:
                to = piece * pitch + low - piece * SEG_ROWS
                stage[to : to + high - low] = part[low - at * third : high - at * third]
        while (done + 1) * SEG_ROWS <= (at + 1) * third:
            here = stage.at[pl.ds(done * pitch, pitch)]
            mine, to = order_ref[2 * SEGS + done // SEGS], order_ref[done]
            keep = pltpu.make_async_copy(here, keep_out.at[to], sems.at[done])
            send = pltpu.make_async_copy(here, send_out.at[to], sems.at[done])
            pl.when(mine == 1)(keep.start)
            pl.when(mine == 0)(send.start)
            pending.append(keep)
            done += 1
    for copy in pending:
        copy.wait()


def image_head_kernel(
    order_ref, feat_in, far_in, pg_in, far_pg_in, slab_ref, keep_out, send_out,
    feat, pg, stage, sems, out_sems,
):
    copies = [
        pltpu.make_async_copy(pg_in, pg.at[pl.ds(0, ROWS)], sems.at[0]),
        pltpu.make_async_copy(feat_in, feat.at[pl.ds(0, ROWS)], sems.at[1]),
        pltpu.make_async_copy(far_pg_in, pg.at[pl.ds(ROWS, ROWS)], sems.at[2]),
        pltpu.make_async_copy(far_in, feat.at[pl.ds(ROWS, ROWS)], sems.at[3]),
    ]
    for copy in copies:
        copy.start()
    for copy in copies:
        copy.wait()
    for piece in range(2 * SEGS):
        low = piece * (SEG_ROWS + SLAB) + SEG_ROWS
        stage[low : low + SLAB] = slab_ref[...]
    head_part(order_ref, feat, pg[...], stage, keep_out, send_out, out_sems)


def image_head(*operands):
    both = pltpu.VMEM((2 * ROWS, WIDTH), bf16)
    return pl.pallas_call(
        image_head_kernel,
        in_specs=[SM] + [HBM] * 4 + [VM],
        out_specs=[HBM] * 2,
        out_shape=[IMG_PIECES, IMG_PIECES],
        scratch_shapes=[both, both, pltpu.VMEM((2 * SEGS * (SEG_ROWS + SLAB), WIDTH), bf16)]
        + [pltpu.SemaphoreType.DMA((4,)), pltpu.SemaphoreType.DMA((2 * SEGS,))],
        compiler_params=pltpu.CompilerParams(vmem_limit_bytes=28 * MIB),
        cost_estimate=cost(4 * ROWS * WIDTH * WIDTH),
    )(*operands)


def text_head_kernel(
    order_ref, feat_in, far_in, emb_in, far_emb_in, recip_in, far_recip_in, gt_in, gft_in, got_in,
    pg_out, far_pg_out, keep_out, send_out,
    feat, emb, recip, grad, got, pg, stage, sems, out_sems, pg_sems,
):
    low, high = pl.ds(0, ROWS), pl.ds(ROWS, ROWS)
    pairs = [
        (gt_in, grad.at[0]), (emb_in, emb.at[0]), (got_in.at[0], got.at[0]), (recip_in, recip.at[0]),
        (gft_in, grad.at[1]), (far_emb_in, emb.at[1]), (got_in.at[1], got.at[1]), (far_recip_in, recip.at[1]),
        (feat_in, feat.at[low]), (far_in, feat.at[high]),
    ]
    copies = [
        pltpu.make_async_copy(source, target, sems.at[at]) for at, (source, target) in enumerate(pairs)
    ]
    for copy in copies:
        copy.start()
    outs = []
    for at, rows in enumerate((low, high)):
        for copy in copies[4 * at : 4 * at + 4]:
            copy.wait()
        pg[rows] = proj_grad(emb[at], recip[at], grad[at] + got[at].astype(f32))
        out = pltpu.make_async_copy(pg.at[rows], (pg_out, far_pg_out)[at], pg_sems.at[at])
        out.start()
        outs.append(out)
    for copy in copies[8:]:
        copy.wait()
    head_part(order_ref, feat, pg[...], stage, keep_out, send_out, out_sems)
    for out in outs:
        out.wait()


def text_head(*operands):
    both, tall = pltpu.VMEM((2 * ROWS, WIDTH), bf16), pltpu.VMEM((2, ROWS, WIDTH), bf16)
    return pl.pallas_call(
        text_head_kernel,
        in_specs=[SM] + [HBM] * 9,
        out_specs=[HBM] * 4,
        out_shape=[FLAT, FLAT, TXT_PIECES, TXT_PIECES],
        scratch_shapes=[both, tall, pltpu.VMEM((2, ROWS, LANES), f32), pltpu.VMEM((2, ROWS, WIDTH), f32),
            tall, both, pltpu.VMEM((WIDTH, WIDTH), bf16)]
        + [pltpu.SemaphoreType.DMA((10,)), pltpu.SemaphoreType.DMA((2 * SEGS,)), pltpu.SemaphoreType.DMA((2,))],
        compiler_params=pltpu.CompilerParams(vmem_limit_bytes=36 * MIB),
        cost_estimate=cost(4 * ROWS * WIDTH * WIDTH),
    )(*operands)


def widen_kernel(order_ref, own_lo, own_hi, their_lo, their_hi, total_out, pieces, stage, sems, out_sems):
    half = SEGS // 2
    copies = []
    for at, source in enumerate((own_lo, own_hi, their_lo, their_hi)):
        target = pieces.at[at // 2, pl.ds(at % 2 * half, half)]
        copies.append(pltpu.make_async_copy(source, target, sems.at[at]))
        copies[-1].start()
    for copy in copies:
        copy.wait()
    outs = []
    for at in range(2 * SEGS):
        side = 1 - order_ref[2 * SEGS + at // SEGS]
        stage[at] = pieces[side, order_ref[at]][:SEG_ROWS].astype(f32)
        outs.append(pltpu.make_async_copy(
            stage.at[at], total_out.at[pl.ds(at * SEG_ROWS, SEG_ROWS)], out_sems.at[at]
        ))
        outs[-1].start()
    for out in outs:
        out.wait()


def widen(order, *parts):
    shape = (2, SEGS, parts[0].shape[1], WIDTH)
    return pl.pallas_call(
        widen_kernel,
        in_specs=[SM] + [HBM] * 4,
        out_specs=HBM,
        out_shape=jax.ShapeDtypeStruct((WIDTH, WIDTH), f32),
        scratch_shapes=[
            pltpu.VMEM(shape, bf16),
            pltpu.VMEM((2 * SEGS, SEG_ROWS, WIDTH), f32),
            pltpu.SemaphoreType.DMA((4,)),
            pltpu.SemaphoreType.DMA((2 * SEGS,)),
        ],
        compiler_params=pltpu.CompilerParams(vmem_limit_bytes=20 * MIB),
        cost_estimate=cost(1_000_000),
    )(order, *parts)


def feature_grad(part, got, weight):
    total = (part.astype(f32) + got.astype(f32)).astype(bf16)
    return lax.dot_general(
        total, weight, (((1,), (1,)), ((), ())), preferred_element_type=f32
    ).astype(bf16)


def per_device(img_feat, txt_feat, text_pair, w_img, w_txt, logit_scale, logit_bias):
    dp, inner = lax.axis_index("dp"), lax.axis_index("inner")
    place = {"x": inner % 4, "y": inner // 4 * 2 + dp // 2 % 2, "z": dp // 4, "core": dp % 2}
    slot = (dp * 8 + inner).astype(jnp.int32).reshape(1)
    orders = [piece_order(place, chain) for chain in range(2)]
    mult = jnp.exp(logit_scale[0])
    scale = jnp.stack([mult * LOG2E, logit_bias[0] * LOG2E, mult])
    pair = (text_pair % ROWS)[None, :]

    far_txt_feat = exchange(txt_feat, over_y)
    far_img_feat = exchange(img_feat, over_z)
    txt_emb, txt_recip = project(txt_feat, w_txt)
    other_emb = exchange(txt_emb, over_core)
    img_emb, img_recip = project(img_feat, w_img)
    grad_img, grad_txt, grad_other, near_loss = near_pairs(scale, pair, img_emb, txt_emb, other_emb)
    (far_txt_feat, far_img_feat, grad_img, grad_txt, grad_other, near_loss, slot, *orders) = (
        lax.optimization_barrier(
            (far_txt_feat, far_img_feat, grad_img, grad_txt, grad_other, near_loss, slot, *orders)
        )
    )

    far_txt_emb, far_txt_recip = project(far_txt_feat, w_txt)
    far_other_emb = exchange(far_txt_emb, over_core)
    far_img_emb, far_img_recip = project(far_img_feat, w_img)
    img_pg, far_img_pg, grad_txt, grad_far_txt, grad_other, slab = far_pairs(
        scale, img_emb, far_img_emb, txt_emb, other_emb, far_txt_emb, far_other_emb,
        img_recip, far_img_recip, grad_img, grad_txt, grad_other, near_loss, slot,
    )
    got_grad = exchange(grad_other, over_core)
    img_got = exchange(far_img_pg, over_z)
    img_keep, img_send = image_head(orders[0], img_feat, far_img_feat, img_pg, far_img_pg, slab)
    img_more = exchange(img_send, over_core)
    txt_pg, far_txt_pg, txt_keep, txt_send = text_head(
        orders[1], txt_feat, far_txt_feat, txt_emb, far_txt_emb,
        txt_recip, far_txt_recip, grad_txt, grad_far_txt, got_grad,
    )
    img_more, txt_keep, txt_send = lax.optimization_barrier((img_more, txt_keep, txt_send))
    txt_got = exchange(far_txt_pg, over_y)
    txt_more = exchange(txt_send, over_core)

    held = [img_keep + img_more, txt_keep + txt_more]
    half = SEGS // 2
    got, _ = over_chain([part[half:] for part in held], 0)
    held = [part[:half] + more for part, more in zip(held, got)]
    got, _ = over_chain([part[1:] for part in held], 1)
    held = [part[:1] + more for part, more in zip(held, got)]
    for step in range(2, len(STEPS)):
        got, _ = over_chain(held, step)
        held = [part + more for part, more in zip(held, got)]
    loss_sum = jnp.sum(held[0][0, SEG_ROWS:].astype(f32))
    got, (img_got, txt_got) = over_chain(held, 1, (img_got, txt_got))
    low = [jnp.concatenate([part, more]) for part, more in zip(held, got)]
    grad_img_feat = feature_grad(img_pg, img_got, w_img)
    grad_txt_feat = feature_grad(txt_pg, txt_got, w_txt)
    high, (grad_img_feat, grad_txt_feat) = over_chain(low, 0, (grad_img_feat, grad_txt_feat))
    grads = [
        widen(order, lo, hi, exchange(lo, over_core), exchange(hi, over_core))
        for order, lo, hi in zip(orders, low, high)
    ]
    loss_mean = (loss_sum / (ROWS * COUNT * ROUNDS)).reshape(1)
    return (grad_img_feat, grad_txt_feat, *grads, loss_mean)


def solution(mesh):
    return jax.shard_map(
        per_device,
        mesh=mesh,
        in_specs=(
            P(("dp", "inner"), None),
            P(("dp", "inner"), None),
            P(("dp", "inner")),
            P(),
            P(),
            P(),
            P(),
        ),
        out_specs=(P(("dp", "inner"), None), P(("dp", "inner"), None), P(), P(), P()),
        check_vma=False,
    )
```

```python
import jax
import jax.numpy as jnp
from jax import lax
from jax.experimental import pallas as pl
from jax.experimental.pallas import tpu as pltpu
from jax.sharding import PartitionSpec as P

AXES = ("dp", "inner")
COUNT = 128
ROUNDS = 8
ROWS, WIDTH, LANES = 512, 1152, 128
CHAINS, PART = 3, 384
SEGS, SEG_ROWS, SLAB = 4, 144, 16
MIB = 1024 * 1024
LOG2E = 1.4426950408889634
bf16, f32 = jnp.bfloat16, jnp.float32
VM = pl.BlockSpec(memory_space=pltpu.VMEM)
SM = pl.BlockSpec(memory_space=pltpu.SMEM)
HBM = pl.BlockSpec(memory_space=pl.ANY)
TALL = jax.ShapeDtypeStruct((2, ROWS, WIDTH), bf16)
FLAT = jax.ShapeDtypeStruct((ROWS, WIDTH), bf16)
WIDE = jax.ShapeDtypeStruct((ROWS, WIDTH), f32)
LOSS = jax.ShapeDtypeStruct((1, ROWS), f32)
RECIP = jax.ShapeDtypeStruct((ROWS, LANES), f32)
SLAB_SHAPE = jax.ShapeDtypeStruct((SLAB, PART), bf16)
PIECES = jax.ShapeDtypeStruct((CHAINS, SEGS, SEG_ROWS, PART), bf16)


def place_of(index):
    dp, inner = index // 8, index % 8
    return {
        "x": inner % 4,
        "y": inner // 4 * 2 + dp // 2 % 2,
        "z": dp // 4,
        "core": dp % 2,
    }


def index_of(place):
    dp = place["z"] * 4 + place["y"] % 2 * 2 + place["core"]
    return dp * 8 + place["y"] // 2 * 4 + place["x"]


def flipped(index, axis, mask):
    place = place_of(index)
    place[axis] ^= mask
    return index_of(place)


def exchange(block, partner):
    return lax.ppermute(block, AXES, [(index, partner(index)) for index in range(COUNT)])


def over_z(index):
    return flipped(index, "z", 1)


def over_y(index):
    return flipped(index, "y", 1)


def over_core(index):
    return flipped(index, "core", 1)


STEPS = (("x", 1), ("x", 3), ("y", 3), ("z", 3), ("y", 1), ("z", 1))


STEPS = (("x", 1), ("x", 3), ("y", 3), ("z", 3), ("y", 1), ("z", 1))


def step_of(core, chain, step):
    return STEPS[(core * CHAINS + chain + step) % len(STEPS)]


def chain_partner(chain, step):
    def partner(index):
        axis, mask = step_of(place_of(index)["core"], chain, step)
        return flipped(index, axis, mask)

    return partner


def my_bit(place, axis, mask):
    high = place[axis] >> 1
    return high if mask == 3 else (place[axis] & 1) ^ high


def segment_of(place, core, chain):
    first = my_bit(place, *step_of(core, chain, 0))
    second = my_bit(place, *step_of(core, chain, 1))
    return 2 * first + second


def piece_order(place):
    order = []
    for chain in range(CHAINS):
        for core in range(2):
            order += [at ^ segment_of(place, core, chain) for at in range(SEGS)]
    order += [(place["core"] == core).astype(jnp.int32) for core in range(2)]
    return jnp.stack(order).astype(jnp.int32)


def over_chain(block, chain, step):
    return exchange(block, chain_partner(chain, step))


def cost(flops):
    return pl.CostEstimate(flops=flops // 100, bytes_accessed=1, transcendentals=0)


def project_kernel(feat_ref, weight_ref, emb_ref, recip_ref):
    projected = jnp.dot(feat_ref[...], weight_ref[...], preferred_element_type=f32)
    recip = lax.rsqrt(jnp.sum(projected * projected, axis=1, keepdims=True) + 1e-06)
    emb_ref[...] = (projected * recip).astype(bf16)
    recip_ref[...] = jnp.broadcast_to(recip, recip_ref.shape)


def project(features, weight, limit=16):
    return pl.pallas_call(
        project_kernel,
        in_specs=[VM, VM],
        out_specs=[VM, VM],
        out_shape=[FLAT, RECIP],
        compiler_params=pltpu.CompilerParams(vmem_limit_bytes=limit << 20),
        cost_estimate=cost(2 * ROWS * WIDTH * WIDTH),
    )(features, weight)


def pair_job(image, text, scale_ref, positive):
    score = lax.dot_general(image, text, (((1,), (1,)), ((), ())), preferred_element_type=f32)
    score = score * scale_ref[0] + scale_ref[1]
    if positive is not None:
        score = jnp.where(positive, -score, score)
    power = jnp.exp2(score)
    whole = power + 1.0
    coefficient = (power * scale_ref[2]) * pl.reciprocal(whole, approx=True)
    if positive is not None:
        coefficient = jnp.where(positive, -coefficient, coefficient)
    quarter = whole.shape[0] // 4
    product = (whole[:quarter] * whole[quarter : 2 * quarter]) * (
        whole[2 * quarter : 3 * quarter] * whole[3 * quarter :]
    )
    loss = jnp.sum(jnp.log(product), axis=0, keepdims=True)
    return loss, coefficient.astype(bf16)


def times_text(coefficient, text):
    return jnp.dot(coefficient, text, preferred_element_type=f32)


def times_image(coefficient, image):
    return lax.dot_general(
        coefficient, image, (((0,), (0,)), ((), ())), preferred_element_type=f32
    )


def proj_grad(emb, recip, grad):
    emb = emb.astype(f32)
    along = jnp.sum(emb * grad, axis=1, keepdims=True)
    return (recip[:, :1] * (grad - emb * along)).astype(bf16)


def near_kernel(
    scale_ref, pair_ref, img, txt, other_lo, other_hi, gi, gt, go, other, loss_ref
):
    rows = img.shape[0]
    positive = pair_ref[...] == lax.broadcasted_iota(jnp.int32, (rows, rows), 0)
    loss, coefficient = pair_job(img[...], txt[...], scale_ref, positive)
    gt[...] = times_image(coefficient, img[...])
    gi[...] = times_text(coefficient, txt[...])
    other[: rows // 2] = other_lo[...]
    other[rows // 2 :] = other_hi[...]
    more, coefficient = pair_job(img[...], other[...], scale_ref, None)
    go[...] = times_image(coefficient, img[...])
    gi[...] += times_text(coefficient, other[...])
    loss_ref[...] = loss + more


def near_pairs(*operands):
    return pl.pallas_call(
        near_kernel,
        in_specs=[SM] + [VM] * 5,
        out_specs=[VM] * 5,
        out_shape=[WIDE, WIDE, WIDE, FLAT, LOSS],
        compiler_params=pltpu.CompilerParams(vmem_limit_bytes=20 * MIB),
        cost_estimate=cost(12 * ROWS * ROWS * WIDTH),
    )(*operands)


def far_kernel(
    scale_ref, img, far, txt, other, far_txt, far_other, recip, far_recip,
    gi_in, gt_in, go_in, near_loss_ref, slot_ref,
    pg, far_pg, gt, gft, send, slab_ref, gi, gf,
):
    loss, last = pair_job(far[...], other[...], scale_ref, None)
    more, first = pair_job(img[...], far_other[...], scale_ref, None)
    loss += more
    send[0] = (go_in[...] + times_image(last, far[...])).astype(bf16)
    gf[...] = times_text(last, other[...])
    more, second = pair_job(far[...], far_other[...], scale_ref, None)
    loss += more
    gi[...] = gi_in[...] + times_text(first, far_other[...])
    send[1] = (times_image(first, img[...]) + times_image(second, far[...])).astype(bf16)
    more, last = pair_job(far[...], txt[...], scale_ref, None)
    loss += more
    gf[...] += times_text(second, far_other[...])
    more, first = pair_job(img[...], far_txt[...], scale_ref, None)
    loss += more
    gt[...] = gt_in[...] + times_image(last, far[...])
    gf[...] += times_text(last, txt[...])
    more, second = pair_job(far[...], far_txt[...], scale_ref, None)
    loss += more
    slab_ref[...] = loss_slab(loss + near_loss_ref[...], slot_ref[0])
    gi[...] += times_text(first, far_txt[...])
    pg[...] = proj_grad(img[...], recip[...], gi[...])
    gf[...] += times_text(second, far_txt[...])
    far_pg[...] = proj_grad(far[...], far_recip[...], gf[...])
    gft[...] = times_image(first, img[...]) + times_image(second, far[...])


def loss_slab(loss, slot):
    loss = jnp.sum(loss, axis=1, keepdims=True)
    high = loss.astype(bf16).astype(f32)
    rest = loss - high
    middle = rest.astype(bf16).astype(f32)
    low = rest - middle
    lane = lax.broadcasted_iota(jnp.int32, (SLAB, PART), 1)
    row = lax.broadcasted_iota(jnp.int32, (SLAB, PART), 0)
    at = jnp.where(row == 0, lane - 3 * slot, -1)
    slab = jnp.where(at == 0, high, jnp.where(at == 1, middle, jnp.where(at == 2, low, 0.0)))
    return slab.astype(bf16)


def far_pairs(*operands):
    return pl.pallas_call(
        far_kernel,
        in_specs=[SM] + [VM] * 12 + [SM],
        out_specs=[VM] * 6,
        out_shape=[FLAT, FLAT, WIDE, WIDE, TALL, SLAB_SHAPE],
        scratch_shapes=[pltpu.VMEM((ROWS, WIDTH), f32), pltpu.VMEM((ROWS, WIDTH), f32)],
        compiler_params=pltpu.CompilerParams(vmem_limit_bytes=24 * MIB),
        cost_estimate=cost(36 * ROWS * ROWS * WIDTH),
    )(*operands)


def head_part(order_ref, feat, far_feat, pg, far_pg, stage, keep_ref, send_ref):
    across = (((0,), (0,)), ((), ()))
    for at in range(0, WIDTH, PART):
        part = lax.dot_general(feat[:, at : at + PART], pg, across, preferred_element_type=f32)
        part += lax.dot_general(
            far_feat[:, at : at + PART], far_pg, across, preferred_element_type=f32
        )
        stage[at : at + PART] = part.astype(bf16)

    def store(out_ref, half):
        for chain in range(CHAINS):
            for at in range(SEGS * half, SEGS * half + SEGS):
                piece = stage[at * SEG_ROWS : (at + 1) * SEG_ROWS, chain * PART : (chain + 1) * PART]
                out_ref[chain, order_ref[2 * SEGS * chain + at]] = piece

    for half in range(2):
        mine = order_ref[2 * SEGS * CHAINS + half] == 1

        @pl.when(mine)
        def _():
            store(keep_ref, half)

        @pl.when(jnp.logical_not(mine))
        def _():
            store(send_ref, half)


def image_head_kernel(order_ref, feat, far_feat, pg, far_pg, keep_ref, send_ref, stage):
    head_part(order_ref, feat, far_feat, pg[...], far_pg[...], stage, keep_ref, send_ref)


def image_head(*operands):
    return pl.pallas_call(
        image_head_kernel,
        in_specs=[SM] + [VM] * 4,
        out_specs=[VM] * 2,
        out_shape=[PIECES, PIECES],
        scratch_shapes=[pltpu.VMEM((WIDTH, WIDTH), bf16)],
        compiler_params=pltpu.CompilerParams(vmem_limit_bytes=16 * MIB),
        cost_estimate=cost(4 * ROWS * WIDTH * WIDTH),
    )(*operands)


def text_head_kernel(
    order_ref, feat, far_feat, emb, far_emb, recip, far_recip, gt, gft, got,
    pg, far_pg, keep_ref, send_ref, stage,
):
    pg[...] = proj_grad(emb[...], recip[...], gt[...] + got[0].astype(f32))
    far_pg[...] = proj_grad(far_emb[...], far_recip[...], gft[...] + got[1].astype(f32))
    head_part(order_ref, feat, far_feat, pg[...], far_pg[...], stage, keep_ref, send_ref)


def text_head(*operands):
    return pl.pallas_call(
        text_head_kernel,
        in_specs=[SM] + [VM] * 9,
        out_specs=[VM] * 4,
        out_shape=[FLAT, FLAT, PIECES, PIECES],
        scratch_shapes=[pltpu.VMEM((WIDTH, WIDTH), bf16)],
        compiler_params=pltpu.CompilerParams(vmem_limit_bytes=16 * MIB),
        cost_estimate=cost(4 * ROWS * WIDTH * WIDTH),
    )(*operands)


def widen_kernel(order_ref, *refs):
    parts, (img_out, txt_out, stage, sems) = refs[: 4 * CHAINS], refs[4 * CHAINS :]
    own, their = parts[: 2 * CHAINS], parts[2 * CHAINS :]
    copies = []

    def fill(sources, chain, matrix, at):
        rows = pl.ds(matrix * SEG_ROWS, SEG_ROWS)
        columns = pl.ds(chain * PART, PART)
        position = order_ref[2 * SEGS * chain + at]
        pair, within = position // 2, position % 2
        for high in range(2):

            @pl.when(pair == high)
            def _():
                piece = sources[CHAINS * high + chain][within, rows]
                stage[matrix, at, :, columns] = piece.astype(f32)

    for half in range(2):
        mine = order_ref[2 * SEGS * CHAINS + half] == 1
        for matrix, out in enumerate((img_out, txt_out)):
            for at in range(SEGS * half, SEGS * half + SEGS):

                @pl.when(mine)
                def _():
                    for chain in range(CHAINS):
                        fill(own, chain, matrix, at)

                @pl.when(jnp.logical_not(mine))
                def _():
                    for chain in range(CHAINS):
                        fill(their, chain, matrix, at)

                copies.append(pltpu.make_async_copy(
                    stage.at[matrix, at], out.at[pl.ds(at * SEG_ROWS, SEG_ROWS)], sems.at[matrix, at]
                ))
                copies[-1].start()
    for copy in copies:
        copy.wait()


def widen(order, *parts):
    return pl.pallas_call(
        widen_kernel,
        in_specs=[SM] + [VM] * (4 * CHAINS),
        out_specs=[HBM] * 2,
        out_shape=[jax.ShapeDtypeStruct((WIDTH, WIDTH), f32)] * 2,
        scratch_shapes=[
            pltpu.VMEM((2, 2 * SEGS, SEG_ROWS, WIDTH), f32),
            pltpu.SemaphoreType.DMA((2, 2 * SEGS)),
        ],
        compiler_params=pltpu.CompilerParams(vmem_limit_bytes=20 * MIB),
        cost_estimate=cost(1_000_000),
    )(order, *parts)


def feature_grad(part, got, weight):
    total = (part.astype(f32) + got.astype(f32)).astype(bf16)
    return lax.dot_general(
        total, weight, (((1,), (1,)), ((), ())), preferred_element_type=f32
    ).astype(bf16)


def per_device(img_feat, txt_feat, text_pair, w_img, w_txt, logit_scale, logit_bias):
    dp, inner = lax.axis_index("dp"), lax.axis_index("inner")
    place = {"x": inner % 4, "y": inner // 4 * 2 + dp // 2 % 2, "z": dp // 4, "core": dp % 2}
    slot = (dp * 8 + inner).astype(jnp.int32).reshape(1)
    order = piece_order(place)
    mult = jnp.exp(logit_scale[0])
    scale = jnp.stack([mult * LOG2E, logit_bias[0] * LOG2E, mult])
    pair = (text_pair % ROWS)[None, :]

    far_txt_feat = exchange(txt_feat, over_y)
    far_img_feat = exchange(img_feat, over_z)
    txt_emb, txt_recip = project(txt_feat, w_txt)
    half = ROWS // 2
    other_lo, other_hi = exchange(txt_emb[:half], over_core), exchange(txt_emb[half:], over_core)
    img_emb, img_recip = project(img_feat, w_img)
    grad_img, grad_txt, grad_other, other_emb, near_loss = near_pairs(
        scale, pair, img_emb, txt_emb, other_lo, other_hi
    )
    (far_txt_feat, far_img_feat, grad_img, grad_txt, grad_other, other_emb, near_loss, slot, order) = (
        lax.optimization_barrier((
            far_txt_feat, far_img_feat, grad_img, grad_txt, grad_other, other_emb, near_loss, slot, order
        ))
    )

    far_txt_emb, far_txt_recip = project(far_txt_feat, w_txt)
    far_other_emb = exchange(far_txt_emb, over_core)
    far_img_emb, far_img_recip = project(far_img_feat, w_img)
    img_pg, far_img_pg, grad_txt, grad_far_txt, grad_other, slab = far_pairs(
        scale, img_emb, far_img_emb, txt_emb, other_emb, far_txt_emb, far_other_emb,
        img_recip, far_img_recip, grad_img, grad_txt, grad_other, near_loss, slot,
    )
    got_grad = exchange(grad_other, over_core)
    slab = slab + exchange(slab, over_core)
    img_got = exchange(far_img_pg, over_z)
    img_keep, img_send = image_head(order, img_feat, far_img_feat, img_pg, far_img_pg)
    img_more = exchange(img_send, over_core)
    txt_pg, far_txt_pg, txt_keep, txt_send = text_head(
        order, txt_feat, far_txt_feat, txt_emb, far_txt_emb,
        txt_recip, far_txt_recip, grad_txt, grad_far_txt, got_grad,
    )
    img_more, slab, txt_keep, txt_send = lax.optimization_barrier(
        (img_more, slab, txt_keep, txt_send)
    )
    txt_got = exchange(far_txt_pg, over_y)
    txt_more = exchange(txt_send, over_core)

    held = []
    slabs = jnp.broadcast_to(slab, (SEGS, SLAB, PART))
    for chain in range(CHAINS):
        rows = [img_keep[chain] + img_more[chain], txt_keep[chain] + txt_more[chain]]
        held.append(jnp.concatenate(rows + [slabs] * (chain == 0), axis=1))
    both = 2 * SEG_ROWS
    low, high = [None] * CHAINS, [None] * CHAINS
    for chain in range(CHAINS):
        block = held[chain]
        block = block[:2] + over_chain(block[2:], chain, 0)
        block = block[:1] + over_chain(block[1:], chain, 1)
        for step in range(2, len(STEPS)):
            block = block + over_chain(block, chain, step)
        if chain == 0:
            loss_sum = jnp.sum(block[0, both:].astype(f32))
            block = block[:, :both]
        got = over_chain(block, chain, 1)
        if chain == 1:
            got, img_got, txt_got = lax.optimization_barrier((got, img_got, txt_got))
        low[chain] = jnp.concatenate([block, got])
        high[chain] = over_chain(low[chain], chain, 0)
    grad_img_feat = feature_grad(img_pg, img_got, w_img)
    grad_txt_feat = feature_grad(txt_pg, txt_got, w_txt)
    own = low + high
    grad_w_img, grad_w_txt = widen(order, *own, *[exchange(part, over_core) for part in own])
    loss_mean = (loss_sum / (ROWS * COUNT * ROUNDS)).reshape(1)
    return (grad_img_feat, grad_txt_feat, grad_w_img, grad_w_txt, loss_mean)


def solution(mesh):
    return jax.shard_map(
        per_device,
        mesh=mesh,
        in_specs=(
            P(("dp", "inner"), None),
            P(("dp", "inner"), None),
            P(("dp", "inner")),
            P(),
            P(),
            P(),
            P(),
        ),
        out_specs=(P(("dp", "inner"), None), P(("dp", "inner"), None), P(), P(), P()),
        check_vma=False,
    )
```

```python
import jax
import jax.numpy as jnp
from jax import lax
from jax.experimental import pallas as pl
from jax.experimental.pallas import tpu as pltpu
from jax.sharding import PartitionSpec as P

AXES = ("dp", "inner")
COUNT = 128
ROUNDS = 8
ROWS, WIDTH, LANES = 512, 1152, 128
CHAINS, PART = 3, 384
SEGS, SEG_ROWS, SLAB = 4, 144, 16
CUTS = (0, 224, 368, 512)
MIB = 1024 * 1024
LOG2E = 1.4426950408889634
bf16, f32 = jnp.bfloat16, jnp.float32
VM = pl.BlockSpec(memory_space=pltpu.VMEM)
SM = pl.BlockSpec(memory_space=pltpu.SMEM)
HBM = pl.BlockSpec(memory_space=pl.ANY)
FLAT = jax.ShapeDtypeStruct((ROWS, WIDTH), bf16)
WIDE = jax.ShapeDtypeStruct((ROWS, WIDTH), f32)
BANDS = [jax.ShapeDtypeStruct((high - low, WIDTH), bf16) for low, high in zip(CUTS, CUTS[1:])]
LOSS = jax.ShapeDtypeStruct((1, ROWS), f32)
RECIP = jax.ShapeDtypeStruct((ROWS, LANES), f32)
SLAB_SHAPE = jax.ShapeDtypeStruct((SLAB, PART), bf16)
PIECES = [jax.ShapeDtypeStruct((SEGS, SEG_ROWS, PART), bf16)] * CHAINS


def place_of(index):
    dp, inner = index // 8, index % 8
    return {
        "x": inner % 4,
        "y": inner // 4 * 2 + dp // 2 % 2,
        "z": dp // 4,
        "core": dp % 2,
    }


def index_of(place):
    dp = place["z"] * 4 + place["y"] % 2 * 2 + place["core"]
    return dp * 8 + place["y"] // 2 * 4 + place["x"]


def flipped(index, axis, mask):
    place = place_of(index)
    place[axis] ^= mask
    return index_of(place)


def exchange(block, partner):
    return lax.ppermute(block, AXES, [(index, partner(index)) for index in range(COUNT)])


def over_z(index):
    return flipped(index, "z", 1)


def over_y(index):
    return flipped(index, "y", 1)


def over_core(index):
    return flipped(index, "core", 1)


STEPS = (("x", 1), ("x", 3), ("y", 3), ("z", 3), ("y", 1), ("z", 1))


STEPS = (("x", 1), ("x", 3), ("y", 3), ("z", 3), ("y", 1), ("z", 1))


def step_of(core, chain, step):
    return STEPS[(core * CHAINS + chain + step) % len(STEPS)]


def chain_partner(chain, step):
    def partner(index):
        axis, mask = step_of(place_of(index)["core"], chain, step)
        return flipped(index, axis, mask)

    return partner


def my_bit(place, axis, mask):
    high = place[axis] >> 1
    return high if mask == 3 else (place[axis] & 1) ^ high


def segment_of(place, core, chain):
    first = my_bit(place, *step_of(core, chain, 0))
    second = my_bit(place, *step_of(core, chain, 1))
    return 2 * first + second


def piece_order(place):
    order = []
    for chain in range(CHAINS):
        for core in range(2):
            order += [at ^ segment_of(place, core, chain) for at in range(SEGS)]
    order += [(place["core"] == core).astype(jnp.int32) for core in range(2)]
    return jnp.stack(order).astype(jnp.int32)


def over_chain(block, chain, step):
    return exchange(block, chain_partner(chain, step))


def cost(flops):
    return pl.CostEstimate(flops=1 + flops // 100, bytes_accessed=1, transcendentals=0)


def project_kernel(feat_ref, weight_ref, emb_ref, recip_ref):
    projected = jnp.dot(feat_ref[...], weight_ref[...], preferred_element_type=f32)
    recip = lax.rsqrt(jnp.sum(projected * projected, axis=1, keepdims=True) + 1e-06)
    emb_ref[...] = (projected * recip).astype(bf16)
    recip_ref[...] = jnp.broadcast_to(recip, recip_ref.shape)


def project(features, weight, limit=16):
    return pl.pallas_call(
        project_kernel,
        in_specs=[VM, VM],
        out_specs=[VM, VM],
        out_shape=[FLAT, RECIP],
        compiler_params=pltpu.CompilerParams(vmem_limit_bytes=limit << 20),
        cost_estimate=cost(2 * ROWS * WIDTH * WIDTH),
    )(features, weight)


def pair_job(image, text, scale_ref, positive):
    score = lax.dot_general(image, text, (((1,), (1,)), ((), ())), preferred_element_type=f32)
    score = score * scale_ref[0] + scale_ref[1]
    if positive is not None:
        score = jnp.where(positive, -score, score)
    power = jnp.exp2(score)
    whole = power + 1.0
    coefficient = (power * scale_ref[2]) * pl.reciprocal(whole, approx=True)
    if positive is not None:
        coefficient = jnp.where(positive, -coefficient, coefficient)
    quarter = whole.shape[0] // 4
    product = (whole[:quarter] * whole[quarter : 2 * quarter]) * (
        whole[2 * quarter : 3 * quarter] * whole[3 * quarter :]
    )
    loss = jnp.sum(jnp.log(product), axis=0, keepdims=True)
    return loss, coefficient.astype(bf16)


def times_text(coefficient, text):
    return jnp.dot(coefficient, text, preferred_element_type=f32)


def times_image(coefficient, image):
    return lax.dot_general(
        coefficient, image, (((0,), (0,)), ((), ())), preferred_element_type=f32
    )


def proj_grad(emb, recip, grad):
    emb = emb.astype(f32)
    along = jnp.sum(emb * grad, axis=1, keepdims=True)
    return (recip[:, :1] * (grad - emb * along)).astype(bf16)


def near_kernel(
    scale_ref, pair_ref, img, txt, other_lo, other_hi, gi, gt, go, other, loss_ref
):
    rows = img.shape[0]
    positive = pair_ref[...] == lax.broadcasted_iota(jnp.int32, (rows, rows), 0)
    loss, coefficient = pair_job(img[...], txt[...], scale_ref, positive)
    gt[...] = times_image(coefficient, img[...])
    gi[...] = times_text(coefficient, txt[...])
    other[: rows // 2] = other_lo[...]
    other[rows // 2 :] = other_hi[...]
    more, coefficient = pair_job(img[...], other[...], scale_ref, None)
    go[...] = times_image(coefficient, img[...])
    gi[...] += times_text(coefficient, other[...])
    loss_ref[...] = loss + more


def near_pairs(*operands):
    return pl.pallas_call(
        near_kernel,
        in_specs=[SM] + [VM] * 5,
        out_specs=[VM] * 5,
        out_shape=[WIDE, WIDE, WIDE, FLAT, LOSS],
        compiler_params=pltpu.CompilerParams(vmem_limit_bytes=20 * MIB),
        cost_estimate=cost(12 * ROWS * ROWS * WIDTH),
    )(*operands)


def far_text_kernel(
    scale_ref, img, far, far_txt, far_other, gi_in, gi, gf, gft, send, loss_ref
):
    loss, first = pair_job(img[...], far_other[...], scale_ref, None)
    more, second = pair_job(far[...], far_other[...], scale_ref, None)
    loss += more
    gi[...] = gi_in[...] + times_text(first, far_other[...])
    gf[...] = times_text(second, far_other[...])
    more, third = pair_job(img[...], far_txt[...], scale_ref, None)
    loss += more
    send[...] = (times_image(first, img[...]) + times_image(second, far[...])).astype(bf16)
    more, fourth = pair_job(far[...], far_txt[...], scale_ref, None)
    loss_ref[...] = loss + more
    gi[...] += times_text(third, far_txt[...])
    gf[...] += times_text(fourth, far_txt[...])
    gft[...] = times_image(third, img[...]) + times_image(fourth, far[...])


def far_text_pairs(*operands):
    return pl.pallas_call(
        far_text_kernel,
        in_specs=[SM] + [VM] * 5,
        out_specs=[VM] * 5,
        out_shape=[WIDE, WIDE, WIDE, FLAT, LOSS],
        compiler_params=pltpu.CompilerParams(vmem_limit_bytes=24 * MIB),
        cost_estimate=cost(24 * ROWS * ROWS * WIDTH),
    )(*operands)


def far_image_kernel(
    scale_ref, img, far, txt, other, recip, far_recip, gi, gf_in, gt_in, go_in,
    near_loss_ref, far_loss_ref, slot_ref,
    pg, far_pg, band_0, band_1, band_2, gt, send, slab_ref, gf,
):
    loss, first = pair_job(far[...], other[...], scale_ref, None)
    pg[...] = proj_grad(img[...], recip[...], gi[...])
    more, second = pair_job(far[...], txt[...], scale_ref, None)
    loss += more
    slab_ref[...] = loss_slab(loss + near_loss_ref[...] + far_loss_ref[...], slot_ref[0])
    gf[...] = gf_in[...] + times_text(first, other[...])
    send[...] = (go_in[...] + times_image(first, far[...])).astype(bf16)
    gf[...] += times_text(second, txt[...])
    far_pg[...] = proj_grad(far[...], far_recip[...], gf[...])
    gt[...] = gt_in[...] + times_image(second, far[...])
    cut_bands(far_pg, (band_0, band_1, band_2))


def cut_bands(whole, bands):
    for low, high, band in zip(CUTS, CUTS[1:], bands):
        band[...] = whole[low:high]


def far_image_pairs(*operands):
    return pl.pallas_call(
        far_image_kernel,
        in_specs=[SM] + [VM] * 12 + [SM],
        out_specs=[VM] * 8,
        out_shape=[FLAT, FLAT, *BANDS, WIDE, FLAT, SLAB_SHAPE],
        scratch_shapes=[pltpu.VMEM((ROWS, WIDTH), f32)],
        compiler_params=pltpu.CompilerParams(vmem_limit_bytes=20 * MIB),
        cost_estimate=cost(12 * ROWS * ROWS * WIDTH),
    )(*operands)


def far_text_grad_kernel(emb, recip, gft, got, far_pg, band_0, band_1, band_2):
    far_pg[...] = proj_grad(emb[...], recip[...], gft[...] + got[...].astype(f32))
    cut_bands(far_pg, (band_0, band_1, band_2))


def far_text_grad(*operands):
    return pl.pallas_call(
        far_text_grad_kernel,
        in_specs=[VM] * 4,
        out_specs=[VM] * 4,
        out_shape=[FLAT, *BANDS],
        compiler_params=pltpu.CompilerParams(vmem_limit_bytes=16 * MIB),
        cost_estimate=cost(1_000_000),
    )(*operands)


def loss_slab(loss, slot):
    loss = jnp.sum(loss, axis=1, keepdims=True)
    high = loss.astype(bf16).astype(f32)
    rest = loss - high
    middle = rest.astype(bf16).astype(f32)
    low = rest - middle
    lane = lax.broadcasted_iota(jnp.int32, (SLAB, PART), 1)
    row = lax.broadcasted_iota(jnp.int32, (SLAB, PART), 0)
    at = jnp.where(row == 0, lane - 3 * slot, -1)
    slab = jnp.where(at == 0, high, jnp.where(at == 1, middle, jnp.where(at == 2, low, 0.0)))
    return slab.astype(bf16)


def head_part(order_ref, feat, far_feat, pg, far_pg, stage, keep, send):
    across = (((0,), (0,)), ((), ()))
    for at in range(0, WIDTH, PART):
        part = lax.dot_general(feat[:, at : at + PART], pg, across, preferred_element_type=f32)
        part += lax.dot_general(
            far_feat[:, at : at + PART], far_pg, across, preferred_element_type=f32
        )
        stage[at : at + PART] = part.astype(bf16)

    def store(outs, half):
        for chain in range(CHAINS):
            for at in range(SEGS * half, SEGS * half + SEGS):
                piece = stage[at * SEG_ROWS : (at + 1) * SEG_ROWS, chain * PART : (chain + 1) * PART]
                outs[chain][order_ref[2 * SEGS * chain + at]] = piece

    for half in range(2):
        mine = order_ref[2 * SEGS * CHAINS + half] == 1

        @pl.when(mine)
        def _():
            store(keep, half)

        @pl.when(jnp.logical_not(mine))
        def _():
            store(send, half)


def image_head_kernel(order_ref, feat, far_feat, pg, far_pg, *refs):
    keep, send, stage = refs[:CHAINS], refs[CHAINS : 2 * CHAINS], refs[2 * CHAINS]
    head_part(order_ref, feat, far_feat, pg[...], far_pg[...], stage, keep, send)


def image_head(*operands):
    return pl.pallas_call(
        image_head_kernel,
        in_specs=[SM] + [VM] * 4,
        out_specs=[VM] * (2 * CHAINS),
        out_shape=PIECES + PIECES,
        scratch_shapes=[pltpu.VMEM((WIDTH, WIDTH), bf16)],
        compiler_params=pltpu.CompilerParams(vmem_limit_bytes=16 * MIB),
        cost_estimate=cost(4 * ROWS * WIDTH * WIDTH),
    )(*operands)


def text_head_kernel(order_ref, feat, far_feat, emb, recip, gt, got, far_pg, pg, *refs):
    keep, send, stage = refs[:CHAINS], refs[CHAINS : 2 * CHAINS], refs[2 * CHAINS]
    pg[...] = proj_grad(emb[...], recip[...], gt[...] + got[...].astype(f32))
    head_part(order_ref, feat, far_feat, pg[...], far_pg[...], stage, keep, send)


def text_head(*operands):
    return pl.pallas_call(
        text_head_kernel,
        in_specs=[SM] + [VM] * 7,
        out_specs=[VM] * (1 + 2 * CHAINS),
        out_shape=[FLAT] + PIECES + PIECES,
        scratch_shapes=[pltpu.VMEM((WIDTH, WIDTH), bf16)],
        compiler_params=pltpu.CompilerParams(vmem_limit_bytes=16 * MIB),
        cost_estimate=cost(4 * ROWS * WIDTH * WIDTH),
    )(*operands)


def widen_kernel(order_ref, *refs):
    parts, (img_out, txt_out, stage, sems) = refs[: 4 * CHAINS], refs[4 * CHAINS :]
    own, their = parts[: 2 * CHAINS], parts[2 * CHAINS :]
    copies = []

    def fill(sources, chain, matrix, at):
        rows = pl.ds(matrix * SEG_ROWS, SEG_ROWS)
        columns = pl.ds(chain * PART, PART)
        position = order_ref[2 * SEGS * chain + at]
        pair, within = position // 2, position % 2
        for high in range(2):

            @pl.when(pair == high)
            def _():
                piece = sources[CHAINS * high + chain][within, rows]
                stage[matrix, at, :, columns] = piece.astype(f32)

    for half in range(2):
        mine = order_ref[2 * SEGS * CHAINS + half] == 1
        for matrix, out in enumerate((img_out, txt_out)):
            for at in range(SEGS * half, SEGS * half + SEGS):

                @pl.when(mine)
                def _():
                    for chain in range(CHAINS):
                        fill(own, chain, matrix, at)

                @pl.when(jnp.logical_not(mine))
                def _():
                    for chain in range(CHAINS):
                        fill(their, chain, matrix, at)

                copies.append(pltpu.make_async_copy(
                    stage.at[matrix, at], out.at[pl.ds(at * SEG_ROWS, SEG_ROWS)], sems.at[matrix, at]
                ))
                copies[-1].start()
    for copy in copies:
        copy.wait()


def widen(order, *parts):
    return pl.pallas_call(
        widen_kernel,
        in_specs=[SM] + [VM] * (4 * CHAINS),
        out_specs=[HBM] * 2,
        out_shape=[jax.ShapeDtypeStruct((WIDTH, WIDTH), f32)] * 2,
        scratch_shapes=[
            pltpu.VMEM((2, 2 * SEGS, SEG_ROWS, WIDTH), f32),
            pltpu.SemaphoreType.DMA((2, 2 * SEGS)),
        ],
        compiler_params=pltpu.CompilerParams(vmem_limit_bytes=20 * MIB),
        cost_estimate=cost(1_000_000),
    )(order, *parts)


def feature_grad(part, got, weight):
    total = (part.astype(f32) + jnp.concatenate(got).astype(f32)).astype(bf16)
    return lax.dot_general(
        total, weight, (((1,), (1,)), ((), ())), preferred_element_type=f32
    ).astype(bf16)


def per_device(img_feat, txt_feat, text_pair, w_img, w_txt, logit_scale, logit_bias):
    dp, inner = lax.axis_index("dp"), lax.axis_index("inner")
    place = {"x": inner % 4, "y": inner // 4 * 2 + dp // 2 % 2, "z": dp // 4, "core": dp % 2}
    slot = (dp * 8 + inner).astype(jnp.int32).reshape(1)
    order = piece_order(place)
    mult = jnp.exp(logit_scale[0])
    scale = jnp.stack([mult * LOG2E, logit_bias[0] * LOG2E, mult])
    pair = (text_pair % ROWS)[None, :]

    far_txt_feat = exchange(txt_feat, over_y)
    far_img_feat = exchange(img_feat, over_z)
    txt_emb, txt_recip = project(txt_feat, w_txt)
    half = ROWS // 2
    other_lo, other_hi = exchange(txt_emb[:half], over_core), exchange(txt_emb[half:], over_core)
    img_emb, img_recip = project(img_feat, w_img)
    grad_img, grad_txt, grad_other, other_emb, near_loss = near_pairs(
        scale, pair, img_emb, txt_emb, other_lo, other_hi
    )
    (far_txt_feat, far_img_feat, grad_img, grad_txt, grad_other, other_emb, near_loss, slot, order) = (
        lax.optimization_barrier((
            far_txt_feat, far_img_feat, grad_img, grad_txt, grad_other, other_emb, near_loss, slot, order
        ))
    )

    far_txt_emb, far_txt_recip = project(far_txt_feat, w_txt)
    far_other_emb = exchange(far_txt_emb, over_core)
    far_img_emb, far_img_recip = project(far_img_feat, w_img)
    grad_img, grad_far, grad_far_txt, far_send, far_loss = far_text_pairs(
        scale, img_emb, far_img_emb, far_txt_emb, far_other_emb, grad_img
    )
    far_got = exchange(far_send, over_core)
    img_pg, far_img_pg, *bands, grad_txt, send, slab = far_image_pairs(
        scale, img_emb, far_img_emb, txt_emb, other_emb, img_recip, far_img_recip,
        grad_img, grad_far, grad_txt, grad_other, near_loss, far_loss, slot,
    )
    got = exchange(send, over_core)
    slab = slab + exchange(slab, over_core)
    img_got = [exchange(band, over_z) for band in bands]
    far_txt_pg, *bands = far_text_grad(far_txt_emb, far_txt_recip, grad_far_txt, far_got)
    txt_got = [exchange(band, over_y) for band in bands]
    far_txt_pg, img_pg, far_img_pg = lax.optimization_barrier((far_txt_pg, img_pg, far_img_pg))
    img_parts = image_head(order, img_feat, far_img_feat, img_pg, far_img_pg)
    img_keep, img_send = img_parts[:CHAINS], img_parts[CHAINS:]
    img_more = [exchange(part, over_core) for part in img_send]
    txt_pg, *txt_parts = text_head(
        order, txt_feat, far_txt_feat, txt_emb, txt_recip, grad_txt, got, far_txt_pg
    )
    img_more, txt_parts, img_got[0], txt_got[0] = lax.optimization_barrier(
        (img_more, txt_parts, img_got[0], txt_got[0])
    )
    txt_keep, txt_send = txt_parts[:CHAINS], txt_parts[CHAINS:]
    txt_more = [exchange(part, over_core) for part in txt_send]
    txt_more, slab = lax.optimization_barrier((txt_more, slab))

    held = []
    slabs = jnp.broadcast_to(slab, (SEGS, SLAB, PART))
    for chain in range(CHAINS):
        rows = [img_keep[chain] + img_more[chain], txt_keep[chain] + txt_more[chain]]
        held.append(jnp.concatenate(rows + [slabs] * (chain == 0), axis=1))
    both = 2 * SEG_ROWS
    low, high = [None] * CHAINS, [None] * CHAINS
    for chain in range(CHAINS):
        block = held[chain]
        block = block[:2] + over_chain(block[2:], chain, 0)
        block = block[:1] + over_chain(block[1:], chain, 1)
        for step in range(2, len(STEPS)):
            got = over_chain(block, chain, step)
            if chain == 0 and step == 3:
                got, img_got[1], txt_got[1] = lax.optimization_barrier((got, img_got[1], txt_got[1]))
            block = block + got
        if chain == 0:
            loss_sum = jnp.sum(block[0, both:].astype(f32))
            block = block[:, :both]
        got = over_chain(block, chain, 1)
        if chain == 0:
            got, img_got[2], txt_got[2] = lax.optimization_barrier((got, img_got[2], txt_got[2]))
        low[chain] = jnp.concatenate([block, got])
        high[chain] = over_chain(low[chain], chain, 0)
    grad_img_feat = feature_grad(img_pg, img_got, w_img)
    grad_txt_feat = feature_grad(txt_pg, txt_got, w_txt)
    *high, grad_img_feat, grad_txt_feat = lax.optimization_barrier(
        (*high, grad_img_feat, grad_txt_feat)
    )
    own = low + high
    grad_w_img, grad_w_txt = widen(order, *own, *[exchange(part, over_core) for part in own])
    loss_mean = (loss_sum / (ROWS * COUNT * ROUNDS)).reshape(1)
    return (grad_img_feat, grad_txt_feat, grad_w_img, grad_w_txt, loss_mean)


def solution(mesh):
    return jax.shard_map(
        per_device,
        mesh=mesh,
        in_specs=(
            P(("dp", "inner"), None),
            P(("dp", "inner"), None),
            P(("dp", "inner")),
            P(),
            P(),
            P(),
            P(),
        ),
        out_specs=(P(("dp", "inner"), None), P(("dp", "inner"), None), P(), P(), P()),
        check_vma=False,
    )
```

```python
import jax
import jax.numpy as jnp
from jax import lax
from jax.experimental import pallas as pl
from jax.experimental.pallas import tpu as pltpu
from jax.sharding import PartitionSpec as P

AXES = ("dp", "inner")
COUNT = 128
ROUNDS = 8
ROWS, WIDTH, LANES = 512, 1152, 128
CHAINS, PART = 3, 384
SEGS, SEG_ROWS, SLAB = 4, 144, 16
CUTS = (0, 224, 368, 512)
MIB = 1024 * 1024
LOG2E = 1.4426950408889634
bf16, f32 = jnp.bfloat16, jnp.float32
VM = pl.BlockSpec(memory_space=pltpu.VMEM)
SM = pl.BlockSpec(memory_space=pltpu.SMEM)
HBM = pl.BlockSpec(memory_space=pl.ANY)
FLAT = jax.ShapeDtypeStruct((ROWS, WIDTH), bf16)
WIDE = jax.ShapeDtypeStruct((ROWS, WIDTH), f32)
BANDS = [jax.ShapeDtypeStruct((high - low, WIDTH), bf16) for low, high in zip(CUTS, CUTS[1:])]
LOSS = jax.ShapeDtypeStruct((1, ROWS), f32)
RECIP = jax.ShapeDtypeStruct((ROWS, LANES), f32)
SLAB_SHAPE = jax.ShapeDtypeStruct((SLAB, PART), bf16)
PIECES = [jax.ShapeDtypeStruct((SEGS, SEG_ROWS, PART), bf16)] * CHAINS


def place_of(index):
    dp, inner = index // 8, index % 8
    return {
        "x": inner % 4,
        "y": inner // 4 * 2 + dp // 2 % 2,
        "z": dp // 4,
        "core": dp % 2,
    }


def index_of(place):
    dp = place["z"] * 4 + place["y"] % 2 * 2 + place["core"]
    return dp * 8 + place["y"] // 2 * 4 + place["x"]


def flipped(index, axis, mask):
    place = place_of(index)
    place[axis] ^= mask
    return index_of(place)


def exchange(block, partner):
    return lax.ppermute(block, AXES, [(index, partner(index)) for index in range(COUNT)])


def over_z(index):
    return flipped(index, "z", 1)


def over_y(index):
    return flipped(index, "y", 1)


def over_core(index):
    return flipped(index, "core", 1)


STEPS = (("x", 1), ("y", 3), ("z", 1), ("x", 3), ("y", 1), ("z", 3))


def step_of(core, chain, step):
    return STEPS[(core * CHAINS + chain + step) % len(STEPS)]


def chain_partner(chain, step):
    def partner(index):
        axis, mask = step_of(place_of(index)["core"], chain, step)
        return flipped(index, axis, mask)

    return partner


def my_bit(place, axis, mask):
    high = place[axis] >> 1
    return high if mask == 3 else (place[axis] & 1) ^ high


def segment_of(place, core, chain):
    first = my_bit(place, *step_of(core, chain, 0))
    second = my_bit(place, *step_of(core, chain, 1))
    return 2 * first + second


def piece_order(place):
    order = []
    for chain in range(CHAINS):
        for core in range(2):
            order += [at ^ segment_of(place, core, chain) for at in range(SEGS)]
    order += [(place["core"] == core).astype(jnp.int32) for core in range(2)]
    return jnp.stack(order).astype(jnp.int32)


def over_chain(block, chain, step):
    return exchange(block, chain_partner(chain, step))


def cost(flops):
    return pl.CostEstimate(flops=1 + flops // 100, bytes_accessed=1, transcendentals=0)


def project_kernel(feat_ref, weight_ref, emb_ref, recip_ref):
    projected = jnp.dot(feat_ref[...], weight_ref[...], preferred_element_type=f32)
    recip = lax.rsqrt(jnp.sum(projected * projected, axis=1, keepdims=True) + 1e-06)
    emb_ref[...] = (projected * recip).astype(bf16)
    recip_ref[...] = jnp.broadcast_to(recip, recip_ref.shape)


def project(features, weight, limit=16):
    return pl.pallas_call(
        project_kernel,
        in_specs=[VM, VM],
        out_specs=[VM, VM],
        out_shape=[FLAT, RECIP],
        compiler_params=pltpu.CompilerParams(vmem_limit_bytes=limit << 20),
        cost_estimate=cost(2 * ROWS * WIDTH * WIDTH),
    )(features, weight)


def pair_job(image, text, scale_ref, positive):
    score = lax.dot_general(image, text, (((1,), (1,)), ((), ())), preferred_element_type=f32)
    score = score * scale_ref[0] + scale_ref[1]
    if positive is not None:
        score = jnp.where(positive, -score, score)
    power = jnp.exp2(score)
    whole = power + 1.0
    coefficient = (power * scale_ref[2]) * pl.reciprocal(whole, approx=True)
    if positive is not None:
        coefficient = jnp.where(positive, -coefficient, coefficient)
    quarter = whole.shape[0] // 4
    product = (whole[:quarter] * whole[quarter : 2 * quarter]) * (
        whole[2 * quarter : 3 * quarter] * whole[3 * quarter :]
    )
    loss = jnp.sum(jnp.log(product), axis=0, keepdims=True)
    return loss, coefficient.astype(bf16)


def times_text(coefficient, text):
    return jnp.dot(coefficient, text, preferred_element_type=f32)


def times_image(coefficient, image):
    return lax.dot_general(
        coefficient, image, (((0,), (0,)), ((), ())), preferred_element_type=f32
    )


def proj_grad(emb, recip, grad):
    emb = emb.astype(f32)
    along = jnp.sum(emb * grad, axis=1, keepdims=True)
    return (recip[:, :1] * (grad - emb * along)).astype(bf16)


def near_kernel(
    scale_ref, pair_ref, img, txt, other_lo, other_hi, gi, gt, go, other, loss_ref
):
    rows = img.shape[0]
    positive = pair_ref[...] == lax.broadcasted_iota(jnp.int32, (rows, rows), 0)
    loss, coefficient = pair_job(img[...], txt[...], scale_ref, positive)
    gt[...] = times_image(coefficient, img[...])
    gi[...] = times_text(coefficient, txt[...])
    other[: rows // 2] = other_lo[...]
    other[rows // 2 :] = other_hi[...]
    more, coefficient = pair_job(img[...], other[...], scale_ref, None)
    go[...] = times_image(coefficient, img[...])
    gi[...] += times_text(coefficient, other[...])
    loss_ref[...] = loss + more


def near_pairs(*operands):
    return pl.pallas_call(
        near_kernel,
        in_specs=[SM] + [VM] * 5,
        out_specs=[VM] * 5,
        out_shape=[WIDE, WIDE, WIDE, FLAT, LOSS],
        compiler_params=pltpu.CompilerParams(vmem_limit_bytes=20 * MIB),
        cost_estimate=cost(12 * ROWS * ROWS * WIDTH),
    )(*operands)


def far_text_kernel(
    scale_ref, img, far, far_txt, far_other, gi_in, gi, gf, gft, send, loss_ref
):
    loss, first = pair_job(img[...], far_other[...], scale_ref, None)
    more, second = pair_job(far[...], far_other[...], scale_ref, None)
    loss += more
    gi[...] = gi_in[...] + times_text(first, far_other[...])
    gf[...] = times_text(second, far_other[...])
    more, third = pair_job(img[...], far_txt[...], scale_ref, None)
    loss += more
    send[...] = (times_image(first, img[...]) + times_image(second, far[...])).astype(bf16)
    more, fourth = pair_job(far[...], far_txt[...], scale_ref, None)
    loss_ref[...] = loss + more
    gi[...] += times_text(third, far_txt[...])
    gf[...] += times_text(fourth, far_txt[...])
    gft[...] = times_image(third, img[...]) + times_image(fourth, far[...])


def far_text_pairs(*operands):
    return pl.pallas_call(
        far_text_kernel,
        in_specs=[SM] + [VM] * 5,
        out_specs=[VM] * 5,
        out_shape=[WIDE, WIDE, WIDE, FLAT, LOSS],
        compiler_params=pltpu.CompilerParams(vmem_limit_bytes=24 * MIB),
        cost_estimate=cost(24 * ROWS * ROWS * WIDTH),
    )(*operands)


def far_image_kernel(
    scale_ref, img, far, txt, other, recip, far_recip, gi, gf_in, gt_in, go_in,
    near_loss_ref, far_loss_ref, slot_ref,
    pg, far_pg, band_0, band_1, band_2, gt, send, slab_ref, gf,
):
    loss, first = pair_job(far[...], other[...], scale_ref, None)
    pg[...] = proj_grad(img[...], recip[...], gi[...])
    more, second = pair_job(far[...], txt[...], scale_ref, None)
    loss += more
    slab_ref[...] = loss_slab(loss + near_loss_ref[...] + far_loss_ref[...], slot_ref[0])
    gf[...] = gf_in[...] + times_text(first, other[...])
    send[...] = (go_in[...] + times_image(first, far[...])).astype(bf16)
    gf[...] += times_text(second, txt[...])
    far_pg[...] = proj_grad(far[...], far_recip[...], gf[...])
    gt[...] = gt_in[...] + times_image(second, far[...])
    cut_bands(far_pg, (band_0, band_1, band_2))


def cut_bands(whole, bands):
    for low, high, band in zip(CUTS, CUTS[1:], bands):
        band[...] = whole[low:high]


def far_image_pairs(*operands):
    return pl.pallas_call(
        far_image_kernel,
        in_specs=[SM] + [VM] * 12 + [SM],
        out_specs=[VM] * 8,
        out_shape=[FLAT, FLAT, *BANDS, WIDE, FLAT, SLAB_SHAPE],
        scratch_shapes=[pltpu.VMEM((ROWS, WIDTH), f32)],
        compiler_params=pltpu.CompilerParams(vmem_limit_bytes=20 * MIB),
        cost_estimate=cost(12 * ROWS * ROWS * WIDTH),
    )(*operands)


def far_text_grad_kernel(emb, recip, gft, got, far_pg, band_0, band_1, band_2):
    far_pg[...] = proj_grad(emb[...], recip[...], gft[...] + got[...].astype(f32))
    cut_bands(far_pg, (band_0, band_1, band_2))


def far_text_grad(*operands):
    return pl.pallas_call(
        far_text_grad_kernel,
        in_specs=[VM] * 4,
        out_specs=[VM] * 4,
        out_shape=[FLAT, *BANDS],
        compiler_params=pltpu.CompilerParams(vmem_limit_bytes=16 * MIB),
        cost_estimate=cost(1_000_000),
    )(*operands)


def loss_slab(loss, slot):
    loss = jnp.sum(loss, axis=1, keepdims=True)
    high = loss.astype(bf16).astype(f32)
    rest = loss - high
    middle = rest.astype(bf16).astype(f32)
    low = rest - middle
    lane = lax.broadcasted_iota(jnp.int32, (SLAB, PART), 1)
    row = lax.broadcasted_iota(jnp.int32, (SLAB, PART), 0)
    at = jnp.where(row == 0, lane - 3 * slot, -1)
    slab = jnp.where(at == 0, high, jnp.where(at == 1, middle, jnp.where(at == 2, low, 0.0)))
    return slab.astype(bf16)


def head_part(order_ref, feat, far_feat, pg, far_pg, stage, keep, send):
    across = (((0,), (0,)), ((), ()))
    for at in range(0, WIDTH, PART):
        part = lax.dot_general(feat[:, at : at + PART], pg, across, preferred_element_type=f32)
        part += lax.dot_general(
            far_feat[:, at : at + PART], far_pg, across, preferred_element_type=f32
        )
        stage[at : at + PART] = part.astype(bf16)

    def store(outs, half):
        for chain in range(CHAINS):
            for at in range(SEGS * half, SEGS * half + SEGS):
                piece = stage[at * SEG_ROWS : (at + 1) * SEG_ROWS, chain * PART : (chain + 1) * PART]
                outs[chain][order_ref[2 * SEGS * chain + at]] = piece

    for half in range(2):
        mine = order_ref[2 * SEGS * CHAINS + half] == 1

        @pl.when(mine)
        def _():
            store(keep, half)

        @pl.when(jnp.logical_not(mine))
        def _():
            store(send, half)


def image_head_kernel(order_ref, feat, far_feat, pg, far_pg, *refs):
    keep, send, stage = refs[:CHAINS], refs[CHAINS : 2 * CHAINS], refs[2 * CHAINS]
    head_part(order_ref, feat, far_feat, pg[...], far_pg[...], stage, keep, send)


def image_head(*operands):
    return pl.pallas_call(
        image_head_kernel,
        in_specs=[SM] + [VM] * 4,
        out_specs=[VM] * (2 * CHAINS),
        out_shape=PIECES + PIECES,
        scratch_shapes=[pltpu.VMEM((WIDTH, WIDTH), bf16)],
        compiler_params=pltpu.CompilerParams(vmem_limit_bytes=16 * MIB),
        cost_estimate=cost(4 * ROWS * WIDTH * WIDTH),
    )(*operands)


def text_head_kernel(order_ref, feat, far_feat, emb, recip, gt, got, far_pg, pg, *refs):
    keep, send, stage = refs[:CHAINS], refs[CHAINS : 2 * CHAINS], refs[2 * CHAINS]
    pg[...] = proj_grad(emb[...], recip[...], gt[...] + got[...].astype(f32))
    head_part(order_ref, feat, far_feat, pg[...], far_pg[...], stage, keep, send)


def text_head(*operands):
    return pl.pallas_call(
        text_head_kernel,
        in_specs=[SM] + [VM] * 7,
        out_specs=[VM] * (1 + 2 * CHAINS),
        out_shape=[FLAT] + PIECES + PIECES,
        scratch_shapes=[pltpu.VMEM((WIDTH, WIDTH), bf16)],
        compiler_params=pltpu.CompilerParams(vmem_limit_bytes=16 * MIB),
        cost_estimate=cost(4 * ROWS * WIDTH * WIDTH),
    )(*operands)


def widen_kernel(order_ref, *refs):
    parts, (img_out, txt_out, stage, sems) = refs[: 4 * CHAINS], refs[4 * CHAINS :]
    own, their = parts[: 2 * CHAINS], parts[2 * CHAINS :]
    copies = []

    def fill(sources, chain, matrix, at):
        rows = pl.ds(matrix * SEG_ROWS, SEG_ROWS)
        columns = pl.ds(chain * PART, PART)
        position = order_ref[2 * SEGS * chain + at]
        pair, within = position // 2, position % 2
        for high in range(2):

            @pl.when(pair == high)
            def _():
                piece = sources[CHAINS * high + chain][within, rows]
                stage[matrix, at, :, columns] = piece.astype(f32)

    for half in range(2):
        mine = order_ref[2 * SEGS * CHAINS + half] == 1
        for matrix, out in enumerate((img_out, txt_out)):
            for at in range(SEGS * half, SEGS * half + SEGS):

                @pl.when(mine)
                def _():
                    for chain in range(CHAINS):
                        fill(own, chain, matrix, at)

                @pl.when(jnp.logical_not(mine))
                def _():
                    for chain in range(CHAINS):
                        fill(their, chain, matrix, at)

                copies.append(pltpu.make_async_copy(
                    stage.at[matrix, at], out.at[pl.ds(at * SEG_ROWS, SEG_ROWS)], sems.at[matrix, at]
                ))
                copies[-1].start()
    for copy in copies:
        copy.wait()


def widen(order, *parts):
    return pl.pallas_call(
        widen_kernel,
        in_specs=[SM] + [VM] * (4 * CHAINS),
        out_specs=[HBM] * 2,
        out_shape=[jax.ShapeDtypeStruct((WIDTH, WIDTH), f32)] * 2,
        scratch_shapes=[
            pltpu.VMEM((2, 2 * SEGS, SEG_ROWS, WIDTH), f32),
            pltpu.SemaphoreType.DMA((2, 2 * SEGS)),
        ],
        compiler_params=pltpu.CompilerParams(vmem_limit_bytes=20 * MIB),
        cost_estimate=cost(1_000_000),
    )(order, *parts)


def feature_grad(part, got, weight):
    total = (part.astype(f32) + jnp.concatenate(got).astype(f32)).astype(bf16)
    return lax.dot_general(
        total, weight, (((1,), (1,)), ((), ())), preferred_element_type=f32
    ).astype(bf16)


def per_device(img_feat, txt_feat, text_pair, w_img, w_txt, logit_scale, logit_bias):
    dp, inner = lax.axis_index("dp"), lax.axis_index("inner")
    place = {"x": inner % 4, "y": inner // 4 * 2 + dp // 2 % 2, "z": dp // 4, "core": dp % 2}
    slot = (dp * 8 + inner).astype(jnp.int32).reshape(1)
    order = piece_order(place)
    mult = jnp.exp(logit_scale[0])
    scale = jnp.stack([mult * LOG2E, logit_bias[0] * LOG2E, mult])
    pair = (text_pair % ROWS)[None, :]

    far_txt_feat = exchange(txt_feat, over_y)
    far_img_feat = exchange(img_feat, over_z)
    txt_emb, txt_recip = project(txt_feat, w_txt)
    half = ROWS // 2
    other_lo, other_hi = exchange(txt_emb[:half], over_core), exchange(txt_emb[half:], over_core)
    img_emb, img_recip = project(img_feat, w_img)
    grad_img, grad_txt, grad_other, other_emb, near_loss = near_pairs(
        scale, pair, img_emb, txt_emb, other_lo, other_hi
    )
    (far_txt_feat, far_img_feat, grad_img, grad_txt, grad_other, other_emb, near_loss, slot, order) = (
        lax.optimization_barrier((
            far_txt_feat, far_img_feat, grad_img, grad_txt, grad_other, other_emb, near_loss, slot, order
        ))
    )

    far_txt_emb, far_txt_recip = project(far_txt_feat, w_txt)
    far_other_emb = exchange(far_txt_emb, over_core)
    far_img_emb, far_img_recip = project(far_img_feat, w_img)
    grad_img, grad_far, grad_far_txt, far_send, far_loss = far_text_pairs(
        scale, img_emb, far_img_emb, far_txt_emb, far_other_emb, grad_img
    )
    far_got = exchange(far_send, over_core)
    img_pg, far_img_pg, *bands, grad_txt, send, slab = far_image_pairs(
        scale, img_emb, far_img_emb, txt_emb, other_emb, img_recip, far_img_recip,
        grad_img, grad_far, grad_txt, grad_other, near_loss, far_loss, slot,
    )
    got = exchange(send, over_core)
    slab = slab + exchange(slab, over_core)
    img_got = [exchange(band, over_z) for band in bands]
    far_txt_pg, *bands = far_text_grad(far_txt_emb, far_txt_recip, grad_far_txt, far_got)
    txt_got = [exchange(band, over_y) for band in bands]
    far_txt_pg, img_pg, far_img_pg = lax.optimization_barrier((far_txt_pg, img_pg, far_img_pg))
    img_parts = image_head(order, img_feat, far_img_feat, img_pg, far_img_pg)
    img_keep, img_send = img_parts[:CHAINS], img_parts[CHAINS:]
    img_more = [exchange(part, over_core) for part in img_send]
    txt_pg, *txt_parts = text_head(
        order, txt_feat, far_txt_feat, txt_emb, txt_recip, grad_txt, got, far_txt_pg
    )
    img_more, txt_parts, img_got[0], txt_got[0] = lax.optimization_barrier(
        (img_more, txt_parts, img_got[0], txt_got[0])
    )
    txt_keep, txt_send = txt_parts[:CHAINS], txt_parts[CHAINS:]
    txt_more = [exchange(part, over_core) for part in txt_send]
    txt_more, slab = lax.optimization_barrier((txt_more, slab))

    held = []
    slabs = jnp.broadcast_to(slab, (SEGS, SLAB, PART))
    for chain in range(CHAINS):
        rows = [img_keep[chain] + img_more[chain], txt_keep[chain] + txt_more[chain]]
        held.append(jnp.concatenate(rows + [slabs] * (chain == 0), axis=1))
    both = 2 * SEG_ROWS
    low, high = [None] * CHAINS, [None] * CHAINS
    for chain in range(CHAINS):
        block = held[chain]
        block = block[:2] + over_chain(block[2:], chain, 0)
        block = block[:1] + over_chain(block[1:], chain, 1)
        for step in range(2, len(STEPS)):
            got = over_chain(block, chain, step)
            if chain == 0 and step == 3:
                got, img_got[1], txt_got[1] = lax.optimization_barrier((got, img_got[1], txt_got[1]))
            block = block + got
        if chain == 0:
            loss_sum = jnp.sum(block[0, both:].astype(f32))
            block = block[:, :both]
        got = over_chain(block, chain, 1)
        low[chain] = jnp.concatenate([block, got])
        high[chain] = over_chain(low[chain], chain, 0)
    grad_img_feat = feature_grad(img_pg, img_got, w_img)
    grad_txt_feat = feature_grad(txt_pg, txt_got, w_txt)
    *high, grad_img_feat, grad_txt_feat = lax.optimization_barrier(
        (*high, grad_img_feat, grad_txt_feat)
    )
    own = low + high
    grad_w_img, grad_w_txt = widen(order, *own, *[exchange(part, over_core) for part in own])
    loss_mean = (loss_sum / (ROWS * COUNT * ROUNDS)).reshape(1)
    return (grad_img_feat, grad_txt_feat, grad_w_img, grad_w_txt, loss_mean)


def solution(mesh):
    return jax.shard_map(
        per_device,
        mesh=mesh,
        in_specs=(
            P(("dp", "inner"), None),
            P(("dp", "inner"), None),
            P(("dp", "inner")),
            P(),
            P(),
            P(),
            P(),
        ),
        out_specs=(P(("dp", "inner"), None), P(("dp", "inner"), None), P(), P(), P()),
        check_vma=False,
    )
```

```python
import jax
import jax.numpy as jnp
from jax import lax
from jax.experimental import pallas as pl
from jax.experimental.pallas import tpu as pltpu
from jax.sharding import PartitionSpec as P

AXES = ("dp", "inner")
COUNT = 128
ROUNDS = 8
ROWS, WIDTH, LANES = 512, 1152, 128
CHAINS, PART = 3, 384
SEGS, SEG_ROWS, SLAB = 4, 144, 16
CUTS = (0, 208, 368, 512)
MIB = 1024 * 1024
LOG2E = 1.4426950408889634
bf16, f32 = jnp.bfloat16, jnp.float32
VM = pl.BlockSpec(memory_space=pltpu.VMEM)
SM = pl.BlockSpec(memory_space=pltpu.SMEM)
HBM = pl.BlockSpec(memory_space=pl.ANY)
FLAT = jax.ShapeDtypeStruct((ROWS, WIDTH), bf16)
WIDE = jax.ShapeDtypeStruct((ROWS, WIDTH), f32)
BANDS = [jax.ShapeDtypeStruct((high - low, WIDTH), bf16) for low, high in zip(CUTS, CUTS[1:])]
LOSS = jax.ShapeDtypeStruct((1, ROWS), f32)
RECIP = jax.ShapeDtypeStruct((ROWS, LANES), f32)
SLAB_SHAPE = jax.ShapeDtypeStruct((SLAB, PART), bf16)
PIECES = [jax.ShapeDtypeStruct((SEGS, SEG_ROWS, PART), bf16)] * CHAINS


def place_of(index):
    dp, inner = index // 8, index % 8
    return {
        "x": inner % 4,
        "y": inner // 4 * 2 + dp // 2 % 2,
        "z": dp // 4,
        "core": dp % 2,
    }


def index_of(place):
    dp = place["z"] * 4 + place["y"] % 2 * 2 + place["core"]
    return dp * 8 + place["y"] // 2 * 4 + place["x"]


def flipped(index, axis, mask):
    place = place_of(index)
    place[axis] ^= mask
    return index_of(place)


def exchange(block, partner):
    return lax.ppermute(block, AXES, [(index, partner(index)) for index in range(COUNT)])


def over_z(index):
    return flipped(index, "z", 1)


def over_y(index):
    return flipped(index, "y", 1)


def over_core(index):
    return flipped(index, "core", 1)


STEPS = (("x", 1), ("y", 3), ("z", 1), ("x", 3), ("y", 1), ("z", 3))


def step_of(core, chain, step):
    return STEPS[(core * CHAINS + chain + step) % len(STEPS)]


def chain_partner(chain, step):
    def partner(index):
        axis, mask = step_of(place_of(index)["core"], chain, step)
        return flipped(index, axis, mask)

    return partner


def my_bit(place, axis, mask):
    high = place[axis] >> 1
    return high if mask == 3 else (place[axis] & 1) ^ high


def segment_of(place, core, chain):
    first = my_bit(place, *step_of(core, chain, 0))
    second = my_bit(place, *step_of(core, chain, 1))
    return 2 * first + second


def piece_order(place):
    order = []
    for chain in range(CHAINS):
        for core in range(2):
            order += [at ^ segment_of(place, core, chain) for at in range(SEGS)]
    order += [(place["core"] == core).astype(jnp.int32) for core in range(2)]
    return jnp.stack(order).astype(jnp.int32)


def over_chain(block, chain, step):
    return exchange(block, chain_partner(chain, step))


def cost(flops):
    return pl.CostEstimate(flops=1 + flops // 100, bytes_accessed=1, transcendentals=0)


def project_kernel(feat_ref, weight_ref, emb_ref, recip_ref):
    projected = jnp.dot(feat_ref[...], weight_ref[...], preferred_element_type=f32)
    recip = lax.rsqrt(jnp.sum(projected * projected, axis=1, keepdims=True) + 1e-06)
    emb_ref[...] = (projected * recip).astype(bf16)
    recip_ref[...] = jnp.broadcast_to(recip, recip_ref.shape)


def project(features, weight, limit=8):
    return pl.pallas_call(
        project_kernel,
        in_specs=[VM, VM],
        out_specs=[VM, VM],
        out_shape=[FLAT, RECIP],
        compiler_params=pltpu.CompilerParams(vmem_limit_bytes=limit << 20),
        cost_estimate=cost(2 * ROWS * WIDTH * WIDTH),
    )(features, weight)


def pair_job(image, text, scale_ref, positive):
    score = lax.dot_general(image, text, (((1,), (1,)), ((), ())), preferred_element_type=f32)
    score = score * scale_ref[0] + scale_ref[1]
    if positive is not None:
        score = jnp.where(positive, -score, score)
    power = jnp.exp2(score)
    whole = power + 1.0
    coefficient = (power * scale_ref[2]) * pl.reciprocal(whole, approx=True)
    if positive is not None:
        coefficient = jnp.where(positive, -coefficient, coefficient)
    quarter = whole.shape[0] // 4
    product = (whole[:quarter] * whole[quarter : 2 * quarter]) * (
        whole[2 * quarter : 3 * quarter] * whole[3 * quarter :]
    )
    loss = jnp.sum(jnp.log(product), axis=0, keepdims=True)
    return loss, coefficient.astype(bf16)


def times_text(coefficient, text):
    return jnp.dot(coefficient, text, preferred_element_type=f32)


def times_image(coefficient, image):
    return lax.dot_general(
        coefficient, image, (((0,), (0,)), ((), ())), preferred_element_type=f32
    )


def proj_grad(emb, recip, grad):
    emb = emb.astype(f32)
    along = jnp.sum(emb * grad, axis=1, keepdims=True)
    return (recip[:, :1] * (grad - emb * along)).astype(bf16)


def near_kernel(
    scale_ref, pair_ref, img, txt, other_lo, other_hi, gi, gt, go, other, loss_ref
):
    rows = img.shape[0]
    positive = pair_ref[...] == lax.broadcasted_iota(jnp.int32, (rows, rows), 0)
    loss, coefficient = pair_job(img[...], txt[...], scale_ref, positive)
    gt[...] = times_image(coefficient, img[...])
    gi[...] = times_text(coefficient, txt[...])
    other[: rows // 2] = other_lo[...]
    other[rows // 2 :] = other_hi[...]
    more, coefficient = pair_job(img[...], other[...], scale_ref, None)
    go[...] = times_image(coefficient, img[...])
    gi[...] += times_text(coefficient, other[...])
    loss_ref[...] = loss + more


def near_pairs(*operands):
    return pl.pallas_call(
        near_kernel,
        in_specs=[SM] + [VM] * 5,
        out_specs=[VM] * 5,
        out_shape=[WIDE, WIDE, WIDE, FLAT, LOSS],
        compiler_params=pltpu.CompilerParams(vmem_limit_bytes=12 * MIB),
        cost_estimate=cost(12 * ROWS * ROWS * WIDTH),
    )(*operands)


def far_text_kernel(
    scale_ref, img, far, far_txt, far_other, gi_in, gi, gf, gft, send, loss_ref
):
    loss, first = pair_job(img[...], far_other[...], scale_ref, None)
    more, second = pair_job(far[...], far_other[...], scale_ref, None)
    loss += more
    gi[...] = gi_in[...] + times_text(first, far_other[...])
    gf[...] = times_text(second, far_other[...])
    more, third = pair_job(img[...], far_txt[...], scale_ref, None)
    loss += more
    send[...] = (times_image(first, img[...]) + times_image(second, far[...])).astype(bf16)
    more, fourth = pair_job(far[...], far_txt[...], scale_ref, None)
    loss_ref[...] = loss + more
    gi[...] += times_text(third, far_txt[...])
    gf[...] += times_text(fourth, far_txt[...])
    gft[...] = times_image(third, img[...]) + times_image(fourth, far[...])


def far_text_pairs(*operands):
    return pl.pallas_call(
        far_text_kernel,
        in_specs=[SM] + [VM] * 5,
        out_specs=[VM] * 5,
        out_shape=[WIDE, WIDE, WIDE, FLAT, LOSS],
        compiler_params=pltpu.CompilerParams(vmem_limit_bytes=14 * MIB),
        cost_estimate=cost(24 * ROWS * ROWS * WIDTH),
    )(*operands)


def far_image_kernel(
    scale_ref, img, far, txt, other, recip, far_recip, gi, gf_in, gt_in, go_in,
    near_loss_ref, far_loss_ref, slot_ref,
    pg, far_pg, band_0, band_1, band_2, gt, send, slab_ref, gf,
):
    loss, first = pair_job(far[...], other[...], scale_ref, None)
    pg[...] = proj_grad(img[...], recip[...], gi[...])
    more, second = pair_job(far[...], txt[...], scale_ref, None)
    loss += more
    slab_ref[...] = loss_slab(loss + near_loss_ref[...] + far_loss_ref[...], slot_ref[0])
    gf[...] = gf_in[...] + times_text(first, other[...])
    send[...] = (go_in[...] + times_image(first, far[...])).astype(bf16)
    gf[...] += times_text(second, txt[...])
    far_pg[...] = proj_grad(far[...], far_recip[...], gf[...])
    gt[...] = gt_in[...] + times_image(second, far[...])
    cut_bands(far_pg, (band_0, band_1, band_2))


def cut_bands(whole, bands):
    for low, high, band in zip(CUTS, CUTS[1:], bands):
        band[...] = whole[low:high]


def far_image_pairs(*operands):
    return pl.pallas_call(
        far_image_kernel,
        in_specs=[SM] + [VM] * 12 + [SM],
        out_specs=[VM] * 8,
        out_shape=[FLAT, FLAT, *BANDS, WIDE, FLAT, SLAB_SHAPE],
        scratch_shapes=[pltpu.VMEM((ROWS, WIDTH), f32)],
        compiler_params=pltpu.CompilerParams(vmem_limit_bytes=12 * MIB),
        cost_estimate=cost(12 * ROWS * ROWS * WIDTH),
    )(*operands)


def far_text_grad_kernel(emb, recip, gft, got, far_pg, band_0, band_1, band_2):
    far_pg[...] = proj_grad(emb[...], recip[...], gft[...] + got[...].astype(f32))
    cut_bands(far_pg, (band_0, band_1, band_2))


def far_text_grad(*operands):
    return pl.pallas_call(
        far_text_grad_kernel,
        in_specs=[VM] * 4,
        out_specs=[VM] * 4,
        out_shape=[FLAT, *BANDS],
        compiler_params=pltpu.CompilerParams(vmem_limit_bytes=8 * MIB),
        cost_estimate=cost(1_000_000),
    )(*operands)


def loss_slab(loss, slot):
    loss = jnp.sum(loss, axis=1, keepdims=True)
    high = loss.astype(bf16).astype(f32)
    rest = loss - high
    middle = rest.astype(bf16).astype(f32)
    low = rest - middle
    lane = lax.broadcasted_iota(jnp.int32, (SLAB, PART), 1)
    row = lax.broadcasted_iota(jnp.int32, (SLAB, PART), 0)
    at = jnp.where(row == 0, lane - 3 * slot, -1)
    slab = jnp.where(at == 0, high, jnp.where(at == 1, middle, jnp.where(at == 2, low, 0.0)))
    return slab.astype(bf16)


def head_part(order_ref, feat, far_feat, pg, far_pg, stage, keep, send):
    across = (((0,), (0,)), ((), ()))
    for at in range(0, WIDTH, PART):
        part = lax.dot_general(feat[:, at : at + PART], pg, across, preferred_element_type=f32)
        part += lax.dot_general(
            far_feat[:, at : at + PART], far_pg, across, preferred_element_type=f32
        )
        stage[at : at + PART] = part.astype(bf16)

    def store(outs, half):
        for chain in range(CHAINS):
            for at in range(SEGS * half, SEGS * half + SEGS):
                piece = stage[at * SEG_ROWS : (at + 1) * SEG_ROWS, chain * PART : (chain + 1) * PART]
                outs[chain][order_ref[2 * SEGS * chain + at]] = piece

    for half in range(2):
        mine = order_ref[2 * SEGS * CHAINS + half] == 1

        @pl.when(mine)
        def _():
            store(keep, half)

        @pl.when(jnp.logical_not(mine))
        def _():
            store(send, half)


def image_head_kernel(order_ref, feat, far_feat, pg, far_pg, *refs):
    keep, send, stage = refs[:CHAINS], refs[CHAINS : 2 * CHAINS], refs[2 * CHAINS]
    head_part(order_ref, feat, far_feat, pg[...], far_pg[...], stage, keep, send)


def image_head(*operands):
    return pl.pallas_call(
        image_head_kernel,
        in_specs=[SM] + [VM] * 4,
        out_specs=[VM] * (2 * CHAINS),
        out_shape=PIECES + PIECES,
        scratch_shapes=[pltpu.VMEM((WIDTH, WIDTH), bf16)],
        compiler_params=pltpu.CompilerParams(vmem_limit_bytes=10 * MIB),
        cost_estimate=cost(4 * ROWS * WIDTH * WIDTH),
    )(*operands)


def text_head_kernel(order_ref, feat, far_feat, emb, recip, gt, got, far_pg, pg, *refs):
    keep, send, stage = refs[:CHAINS], refs[CHAINS : 2 * CHAINS], refs[2 * CHAINS]
    pg[...] = proj_grad(emb[...], recip[...], gt[...] + got[...].astype(f32))
    head_part(order_ref, feat, far_feat, pg[...], far_pg[...], stage, keep, send)


def text_head(*operands):
    return pl.pallas_call(
        text_head_kernel,
        in_specs=[SM] + [VM] * 7,
        out_specs=[VM] * (1 + 2 * CHAINS),
        out_shape=[FLAT] + PIECES + PIECES,
        scratch_shapes=[pltpu.VMEM((WIDTH, WIDTH), bf16)],
        compiler_params=pltpu.CompilerParams(vmem_limit_bytes=12 * MIB),
        cost_estimate=cost(4 * ROWS * WIDTH * WIDTH),
    )(*operands)


def widen_kernel(order_ref, *refs):
    parts, (img_out, txt_out, stage, sems) = refs[: 4 * CHAINS], refs[4 * CHAINS :]
    own, their = parts[: 2 * CHAINS], parts[2 * CHAINS :]
    copies = []

    def fill(sources, chain, matrix, at):
        rows = pl.ds(matrix * SEG_ROWS, SEG_ROWS)
        columns = pl.ds(chain * PART, PART)
        position = order_ref[2 * SEGS * chain + at]
        pair, within = position // 2, position % 2
        for high in range(2):

            @pl.when(pair == high)
            def _():
                piece = sources[CHAINS * high + chain][within, rows]
                stage[matrix, at, :, columns] = piece.astype(f32)

    for half in range(2):
        mine = order_ref[2 * SEGS * CHAINS + half] == 1
        for matrix, out in enumerate((img_out, txt_out)):
            for at in range(SEGS * half, SEGS * half + SEGS):

                @pl.when(mine)
                def _():
                    for chain in range(CHAINS):
                        fill(own, chain, matrix, at)

                @pl.when(jnp.logical_not(mine))
                def _():
                    for chain in range(CHAINS):
                        fill(their, chain, matrix, at)

                copies.append(pltpu.make_async_copy(
                    stage.at[matrix, at], out.at[pl.ds(at * SEG_ROWS, SEG_ROWS)], sems.at[matrix, at]
                ))
                copies[-1].start()
    for copy in copies:
        copy.wait()


def widen(order, *parts):
    return pl.pallas_call(
        widen_kernel,
        in_specs=[SM] + [VM] * (4 * CHAINS),
        out_specs=[HBM] * 2,
        out_shape=[jax.ShapeDtypeStruct((WIDTH, WIDTH), f32)] * 2,
        scratch_shapes=[
            pltpu.VMEM((2, 2 * SEGS, SEG_ROWS, WIDTH), f32),
            pltpu.SemaphoreType.DMA((2, 2 * SEGS)),
        ],
        compiler_params=pltpu.CompilerParams(vmem_limit_bytes=14 * MIB),
        cost_estimate=cost(1_000_000),
    )(order, *parts)


def feature_grad(part, got, weight):
    total = (part.astype(f32) + jnp.concatenate(got).astype(f32)).astype(bf16)
    return lax.dot_general(
        total, weight, (((1,), (1,)), ((), ())), preferred_element_type=f32
    ).astype(bf16)


def per_device(img_feat, txt_feat, text_pair, w_img, w_txt, logit_scale, logit_bias):
    dp, inner = lax.axis_index("dp"), lax.axis_index("inner")
    place = {"x": inner % 4, "y": inner // 4 * 2 + dp // 2 % 2, "z": dp // 4, "core": dp % 2}
    slot = (dp * 8 + inner).astype(jnp.int32).reshape(1)
    order = piece_order(place)
    mult = jnp.exp(logit_scale[0])
    scale = jnp.stack([mult * LOG2E, logit_bias[0] * LOG2E, mult])
    pair = (text_pair % ROWS)[None, :]

    far_txt_feat = exchange(txt_feat, over_y)
    far_img_feat = exchange(img_feat, over_z)
    txt_emb, txt_recip = project(txt_feat, w_txt)
    half = ROWS // 2
    other_lo, other_hi = exchange(txt_emb[:half], over_core), exchange(txt_emb[half:], over_core)
    img_emb, img_recip = project(img_feat, w_img)
    grad_img, grad_txt, grad_other, other_emb, near_loss = near_pairs(
        scale, pair, img_emb, txt_emb, other_lo, other_hi
    )
    (far_txt_feat, far_img_feat, grad_img, grad_txt, grad_other, other_emb, near_loss, slot, order) = (
        lax.optimization_barrier((
            far_txt_feat, far_img_feat, grad_img, grad_txt, grad_other, other_emb, near_loss, slot, order
        ))
    )

    far_txt_emb, far_txt_recip = project(far_txt_feat, w_txt)
    far_other_emb = exchange(far_txt_emb, over_core)
    far_img_emb, far_img_recip = project(far_img_feat, w_img)
    grad_img, grad_far, grad_far_txt, far_send, far_loss = far_text_pairs(
        scale, img_emb, far_img_emb, far_txt_emb, far_other_emb, grad_img
    )
    far_got = exchange(far_send, over_core)
    img_pg, far_img_pg, *bands, grad_txt, send, slab = far_image_pairs(
        scale, img_emb, far_img_emb, txt_emb, other_emb, img_recip, far_img_recip,
        grad_img, grad_far, grad_txt, grad_other, near_loss, far_loss, slot,
    )
    got = exchange(send, over_core)
    slab = slab + exchange(slab, over_core)
    img_got = [exchange(band, over_z) for band in bands]
    far_txt_pg, *bands = far_text_grad(far_txt_emb, far_txt_recip, grad_far_txt, far_got)
    txt_got = [exchange(band, over_y) for band in bands]
    far_txt_pg, img_pg, far_img_pg = lax.optimization_barrier((far_txt_pg, img_pg, far_img_pg))
    img_parts = image_head(order, img_feat, far_img_feat, img_pg, far_img_pg)
    img_keep, img_send = img_parts[:CHAINS], img_parts[CHAINS:]
    img_more = [exchange(part, over_core) for part in img_send]
    txt_pg, *txt_parts = text_head(
        order, txt_feat, far_txt_feat, txt_emb, txt_recip, grad_txt, got, far_txt_pg
    )
    img_more, txt_parts, img_got[0], txt_got[0], slab = lax.optimization_barrier(
        (img_more, txt_parts, img_got[0], txt_got[0], slab)
    )
    txt_keep, txt_send = txt_parts[:CHAINS], txt_parts[CHAINS:]
    txt_more = lax.optimization_barrier([exchange(part, over_core) for part in txt_send])

    held = []
    slabs = jnp.broadcast_to(slab, (SEGS, SLAB, PART))
    for chain in range(CHAINS):
        rows = [img_keep[chain] + img_more[chain], txt_keep[chain] + txt_more[chain]]
        held.append(jnp.concatenate(rows + [slabs] * (chain == 0), axis=1))
    both = 2 * SEG_ROWS
    low, high = [None] * CHAINS, [None] * CHAINS
    for chain in range(CHAINS):
        block = held[chain]
        block = block[:2] + over_chain(block[2:], chain, 0)
        block = block[:1] + over_chain(block[1:], chain, 1)
        for step in range(2, len(STEPS)):
            got = over_chain(block, chain, step)
            if chain == 0 and step == 3:
                got, img_got[1], txt_got[1] = lax.optimization_barrier((got, img_got[1], txt_got[1]))
            block = block + got
        if chain == 0:
            loss_sum = jnp.sum(block[0, both:].astype(f32))
            block = block[:, :both]
        got = over_chain(block, chain, 1)
        low[chain] = jnp.concatenate([block, got])
        high[chain] = over_chain(low[chain], chain, 0)
    grad_img_feat = feature_grad(img_pg, img_got, w_img)
    grad_txt_feat = feature_grad(txt_pg, txt_got, w_txt)
    *high, grad_img_feat, grad_txt_feat = lax.optimization_barrier(
        (*high, grad_img_feat, grad_txt_feat)
    )
    own = low + high
    grad_w_img, grad_w_txt = widen(order, *own, *[exchange(part, over_core) for part in own])
    loss_mean = (loss_sum / (ROWS * COUNT * ROUNDS)).reshape(1)
    return (grad_img_feat, grad_txt_feat, grad_w_img, grad_w_txt, loss_mean)


def solution(mesh):
    return jax.shard_map(
        per_device,
        mesh=mesh,
        in_specs=(
            P(("dp", "inner"), None),
            P(("dp", "inner"), None),
            P(("dp", "inner")),
            P(),
            P(),
            P(),
            P(),
        ),
        out_specs=(P(("dp", "inner"), None), P(("dp", "inner"), None), P(), P(), P()),
        check_vma=False,
    )
```

```python
import jax
import jax.numpy as jnp
from jax import lax
from jax.experimental import pallas as pl
from jax.experimental.pallas import tpu as pltpu
from jax.sharding import PartitionSpec as P

AXES = ("dp", "inner")
COUNT = 128
ROUNDS = 8
ROWS, WIDTH, LANES = 512, 1152, 128
CHAINS, PART = 3, 384
SEGS, SEG_ROWS, SLAB = 4, 144, 16
CUTS = (0, 208, 368, 512)
MIB = 1024 * 1024
LOG2E = 1.4426950408889634
bf16, f32 = jnp.bfloat16, jnp.float32
VM = pl.BlockSpec(memory_space=pltpu.VMEM)
SM = pl.BlockSpec(memory_space=pltpu.SMEM)
HBM = pl.BlockSpec(memory_space=pl.ANY)
FLAT = jax.ShapeDtypeStruct((ROWS, WIDTH), bf16)
WIDE = jax.ShapeDtypeStruct((ROWS, WIDTH), f32)
BANDS = [jax.ShapeDtypeStruct((high - low, WIDTH), bf16) for low, high in zip(CUTS, CUTS[1:])]
LOSS = jax.ShapeDtypeStruct((1, ROWS), f32)
RECIP = jax.ShapeDtypeStruct((ROWS, LANES), f32)
SLAB_SHAPE = jax.ShapeDtypeStruct((SLAB, PART), bf16)
PIECES = [jax.ShapeDtypeStruct((SEGS, SEG_ROWS, PART), bf16)] * CHAINS


def place_of(index):
    dp, inner = index // 8, index % 8
    return {
        "x": inner % 4,
        "y": inner // 4 * 2 + dp // 2 % 2,
        "z": dp // 4,
        "core": dp % 2,
    }


def index_of(place):
    dp = place["z"] * 4 + place["y"] % 2 * 2 + place["core"]
    return dp * 8 + place["y"] // 2 * 4 + place["x"]


def flipped(index, axis, mask):
    place = place_of(index)
    place[axis] ^= mask
    return index_of(place)


def exchange(block, partner):
    return lax.ppermute(block, AXES, [(index, partner(index)) for index in range(COUNT)])


def over_z(index):
    return flipped(index, "z", 1)


def over_y(index):
    return flipped(index, "y", 1)


def over_core(index):
    return flipped(index, "core", 1)


STEPS = (("x", 1), ("y", 3), ("z", 1), ("x", 3), ("y", 1), ("z", 3))


def step_of(core, chain, step):
    return STEPS[(core * CHAINS + chain + step) % len(STEPS)]


def chain_partner(chain, step):
    def partner(index):
        axis, mask = step_of(place_of(index)["core"], chain, step)
        return flipped(index, axis, mask)

    return partner


def my_bit(place, axis, mask):
    high = place[axis] >> 1
    return high if mask == 3 else (place[axis] & 1) ^ high


def segment_of(place, core, chain):
    first = my_bit(place, *step_of(core, chain, 0))
    second = my_bit(place, *step_of(core, chain, 1))
    return 2 * first + second


def piece_order(place):
    order = []
    for chain in range(CHAINS):
        for core in range(2):
            order += [at ^ segment_of(place, core, chain) for at in range(SEGS)]
    order += [(place["core"] == core).astype(jnp.int32) for core in range(2)]
    return jnp.stack(order).astype(jnp.int32)


def over_chain(block, chain, step):
    return exchange(block, chain_partner(chain, step))


def cost(flops):
    return pl.CostEstimate(flops=1 + flops // 100, bytes_accessed=1, transcendentals=0)


def project_kernel(feat_ref, weight_ref, emb_ref, recip_ref):
    projected = jnp.dot(feat_ref[...], weight_ref[...], preferred_element_type=f32)
    recip = lax.rsqrt(jnp.sum(projected * projected, axis=1, keepdims=True) + 1e-06)
    emb_ref[...] = (projected * recip).astype(bf16)
    recip_ref[...] = jnp.broadcast_to(recip, recip_ref.shape)


def project(features, weight, limit=8):
    return pl.pallas_call(
        project_kernel,
        in_specs=[VM, VM],
        out_specs=[VM, VM],
        out_shape=[FLAT, RECIP],
        compiler_params=pltpu.CompilerParams(vmem_limit_bytes=limit << 20),
        cost_estimate=cost(2 * ROWS * WIDTH * WIDTH),
    )(features, weight)


def pair_job(image, text, scale_ref, positive):
    score = lax.dot_general(image, text, (((1,), (1,)), ((), ())), preferred_element_type=f32)
    score = score * scale_ref[0] + scale_ref[1]
    if positive is not None:
        score = jnp.where(positive, -score, score)
    power = jnp.exp2(score)
    whole = power + 1.0
    coefficient = (power * scale_ref[2]) * pl.reciprocal(whole, approx=True)
    if positive is not None:
        coefficient = jnp.where(positive, -coefficient, coefficient)
    quarter = whole.shape[0] // 4
    product = (whole[:quarter] * whole[quarter : 2 * quarter]) * (
        whole[2 * quarter : 3 * quarter] * whole[3 * quarter :]
    )
    loss = jnp.sum(jnp.log(product), axis=0, keepdims=True)
    return loss, coefficient.astype(bf16)


def times_text(coefficient, text):
    return jnp.dot(coefficient, text, preferred_element_type=f32)


def times_image(coefficient, image):
    return lax.dot_general(
        coefficient, image, (((0,), (0,)), ((), ())), preferred_element_type=f32
    )


def proj_grad(emb, recip, grad):
    emb = emb.astype(f32)
    along = jnp.sum(emb * grad, axis=1, keepdims=True)
    return (recip[:, :1] * (grad - emb * along)).astype(bf16)


def near_kernel(
    scale_ref, pair_ref, img, txt, other_lo, other_hi, gi, gt, go, other, loss_ref
):
    rows = img.shape[0]
    positive = pair_ref[...] == lax.broadcasted_iota(jnp.int32, (rows, rows), 0)
    loss, coefficient = pair_job(img[...], txt[...], scale_ref, positive)
    gt[...] = times_image(coefficient, img[...])
    gi[...] = times_text(coefficient, txt[...])
    other[: rows // 2] = other_lo[...]
    other[rows // 2 :] = other_hi[...]
    more, coefficient = pair_job(img[...], other[...], scale_ref, None)
    go[...] = times_image(coefficient, img[...])
    gi[...] += times_text(coefficient, other[...])
    loss_ref[...] = loss + more


def near_pairs(*operands):
    return pl.pallas_call(
        near_kernel,
        in_specs=[SM] + [VM] * 5,
        out_specs=[VM] * 5,
        out_shape=[WIDE, WIDE, WIDE, FLAT, LOSS],
        compiler_params=pltpu.CompilerParams(vmem_limit_bytes=12 * MIB),
        cost_estimate=cost(12 * ROWS * ROWS * WIDTH),
    )(*operands)


def far_text_kernel(
    scale_ref, img, far, far_txt, far_other, gi_in, gi, gf, gft, send, loss_ref
):
    loss, first = pair_job(img[...], far_other[...], scale_ref, None)
    more, second = pair_job(far[...], far_other[...], scale_ref, None)
    loss += more
    gi[...] = gi_in[...] + times_text(first, far_other[...])
    gf[...] = times_text(second, far_other[...])
    more, third = pair_job(img[...], far_txt[...], scale_ref, None)
    loss += more
    send[...] = (times_image(first, img[...]) + times_image(second, far[...])).astype(bf16)
    more, fourth = pair_job(far[...], far_txt[...], scale_ref, None)
    loss_ref[...] = loss + more
    gi[...] += times_text(third, far_txt[...])
    gf[...] += times_text(fourth, far_txt[...])
    gft[...] = times_image(third, img[...]) + times_image(fourth, far[...])


def far_text_pairs(*operands):
    return pl.pallas_call(
        far_text_kernel,
        in_specs=[SM] + [VM] * 5,
        out_specs=[VM] * 5,
        out_shape=[WIDE, WIDE, WIDE, FLAT, LOSS],
        compiler_params=pltpu.CompilerParams(vmem_limit_bytes=14 * MIB),
        cost_estimate=cost(24 * ROWS * ROWS * WIDTH),
    )(*operands)


def far_image_kernel(
    scale_ref, img, far, txt, other, recip, far_recip, gi, gf_in, gt_in, go_in,
    near_loss_ref, far_loss_ref, slot_ref,
    pg, far_pg, band_0, band_1, band_2, gt, send, slab_ref, gf,
):
    loss, first = pair_job(far[...], other[...], scale_ref, None)
    pg[...] = proj_grad(img[...], recip[...], gi[...])
    more, second = pair_job(far[...], txt[...], scale_ref, None)
    loss += more
    slab_ref[...] = loss_slab(loss + near_loss_ref[...] + far_loss_ref[...], slot_ref[0])
    gf[...] = gf_in[...] + times_text(first, other[...])
    send[...] = (go_in[...] + times_image(first, far[...])).astype(bf16)
    gf[...] += times_text(second, txt[...])
    far_pg[...] = proj_grad(far[...], far_recip[...], gf[...])
    gt[...] = gt_in[...] + times_image(second, far[...])
    cut_bands(far_pg, (band_0, band_1, band_2))


def cut_bands(whole, bands):
    for low, high, band in zip(CUTS, CUTS[1:], bands):
        band[...] = whole[low:high]


def far_image_pairs(*operands):
    return pl.pallas_call(
        far_image_kernel,
        in_specs=[SM] + [VM] * 12 + [SM],
        out_specs=[VM] * 8,
        out_shape=[FLAT, FLAT, *BANDS, WIDE, FLAT, SLAB_SHAPE],
        scratch_shapes=[pltpu.VMEM((ROWS, WIDTH), f32)],
        compiler_params=pltpu.CompilerParams(vmem_limit_bytes=12 * MIB),
        cost_estimate=cost(12 * ROWS * ROWS * WIDTH),
    )(*operands)


def far_text_grad_kernel(emb, recip, gft, got, far_pg, band_0, band_1, band_2):
    far_pg[...] = proj_grad(emb[...], recip[...], gft[...] + got[...].astype(f32))
    cut_bands(far_pg, (band_0, band_1, band_2))


def far_text_grad(*operands):
    return pl.pallas_call(
        far_text_grad_kernel,
        in_specs=[VM] * 4,
        out_specs=[VM] * 4,
        out_shape=[FLAT, *BANDS],
        compiler_params=pltpu.CompilerParams(vmem_limit_bytes=8 * MIB),
        cost_estimate=cost(1_000_000),
    )(*operands)


def loss_slab(loss, slot):
    loss = jnp.sum(loss, axis=1, keepdims=True)
    high = loss.astype(bf16).astype(f32)
    rest = loss - high
    middle = rest.astype(bf16).astype(f32)
    low = rest - middle
    lane = lax.broadcasted_iota(jnp.int32, (SLAB, PART), 1)
    row = lax.broadcasted_iota(jnp.int32, (SLAB, PART), 0)
    at = jnp.where(row == 0, lane - 3 * slot, -1)
    slab = jnp.where(at == 0, high, jnp.where(at == 1, middle, jnp.where(at == 2, low, 0.0)))
    return slab.astype(bf16)


def head_part(order_ref, feat, far_feat, pg, far_pg, stage, keep, send):
    across = (((0,), (0,)), ((), ()))
    for at in range(0, WIDTH, PART):
        part = lax.dot_general(feat[:, at : at + PART], pg, across, preferred_element_type=f32)
        part += lax.dot_general(
            far_feat[:, at : at + PART], far_pg, across, preferred_element_type=f32
        )
        stage[at : at + PART] = part.astype(bf16)

    def store(outs, half):
        for chain in range(CHAINS):
            for at in range(SEGS * half, SEGS * half + SEGS):
                piece = stage[at * SEG_ROWS : (at + 1) * SEG_ROWS, chain * PART : (chain + 1) * PART]
                outs[chain][order_ref[2 * SEGS * chain + at]] = piece

    for half in range(2):
        mine = order_ref[2 * SEGS * CHAINS + half] == 1

        @pl.when(mine)
        def _():
            store(keep, half)

        @pl.when(jnp.logical_not(mine))
        def _():
            store(send, half)


def image_head_kernel(order_ref, feat, far_feat, pg, far_pg, *refs):
    keep, send, stage = refs[:CHAINS], refs[CHAINS : 2 * CHAINS], refs[2 * CHAINS]
    head_part(order_ref, feat, far_feat, pg[...], far_pg[...], stage, keep, send)


def image_head(*operands):
    return pl.pallas_call(
        image_head_kernel,
        in_specs=[SM] + [VM] * 4,
        out_specs=[VM] * (2 * CHAINS),
        out_shape=PIECES + PIECES,
        scratch_shapes=[pltpu.VMEM((WIDTH, WIDTH), bf16)],
        compiler_params=pltpu.CompilerParams(vmem_limit_bytes=10 * MIB),
        cost_estimate=cost(4 * ROWS * WIDTH * WIDTH),
    )(*operands)


def text_head_kernel(order_ref, feat, far_feat, emb, recip, gt, got, far_pg, pg, *refs):
    keep, send, stage = refs[:CHAINS], refs[CHAINS : 2 * CHAINS], refs[2 * CHAINS]
    pg[...] = proj_grad(emb[...], recip[...], gt[...] + got[...].astype(f32))
    head_part(order_ref, feat, far_feat, pg[...], far_pg[...], stage, keep, send)


def text_head(*operands):
    return pl.pallas_call(
        text_head_kernel,
        in_specs=[SM] + [VM] * 7,
        out_specs=[VM] * (1 + 2 * CHAINS),
        out_shape=[FLAT] + PIECES + PIECES,
        scratch_shapes=[pltpu.VMEM((WIDTH, WIDTH), bf16)],
        compiler_params=pltpu.CompilerParams(vmem_limit_bytes=12 * MIB),
        cost_estimate=cost(4 * ROWS * WIDTH * WIDTH),
    )(*operands)


def widen_kernel(order_ref, *refs):
    parts, (img_out, txt_out, stage, sems) = refs[: 4 * CHAINS], refs[4 * CHAINS :]
    own, their = parts[: 2 * CHAINS], parts[2 * CHAINS :]
    copies = []

    def fill(sources, chain, matrix, at):
        rows = pl.ds(matrix * SEG_ROWS, SEG_ROWS)
        columns = pl.ds(chain * PART, PART)
        position = order_ref[2 * SEGS * chain + at]
        pair, within = position // 2, position % 2
        for high in range(2):

            @pl.when(pair == high)
            def _():
                piece = sources[CHAINS * high + chain][within, rows]
                stage[matrix, at, :, columns] = piece.astype(f32)

    for half in range(2):
        mine = order_ref[2 * SEGS * CHAINS + half] == 1
        for matrix, out in enumerate((img_out, txt_out)):
            for at in range(SEGS * half, SEGS * half + SEGS):

                @pl.when(mine)
                def _():
                    for chain in range(CHAINS):
                        fill(own, chain, matrix, at)

                @pl.when(jnp.logical_not(mine))
                def _():
                    for chain in range(CHAINS):
                        fill(their, chain, matrix, at)

                copies.append(pltpu.make_async_copy(
                    stage.at[matrix, at], out.at[pl.ds(at * SEG_ROWS, SEG_ROWS)], sems.at[matrix, at]
                ))
                copies[-1].start()
    for copy in copies:
        copy.wait()


def widen(order, *parts):
    return pl.pallas_call(
        widen_kernel,
        in_specs=[SM] + [VM] * (4 * CHAINS),
        out_specs=[HBM] * 2,
        out_shape=[jax.ShapeDtypeStruct((WIDTH, WIDTH), f32)] * 2,
        scratch_shapes=[
            pltpu.VMEM((2, 2 * SEGS, SEG_ROWS, WIDTH), f32),
            pltpu.SemaphoreType.DMA((2, 2 * SEGS)),
        ],
        compiler_params=pltpu.CompilerParams(vmem_limit_bytes=14 * MIB),
        cost_estimate=cost(1_000_000),
    )(order, *parts)


def feature_grad(part, got, weight):
    total = (part.astype(f32) + jnp.concatenate(got).astype(f32)).astype(bf16)
    return lax.dot_general(
        total, weight, (((1,), (1,)), ((), ())), preferred_element_type=f32
    ).astype(bf16)


def per_device(img_feat, txt_feat, text_pair, w_img, w_txt, logit_scale, logit_bias):
    dp, inner = lax.axis_index("dp"), lax.axis_index("inner")
    place = {"x": inner % 4, "y": inner // 4 * 2 + dp // 2 % 2, "z": dp // 4, "core": dp % 2}
    slot = (dp * 8 + inner).astype(jnp.int32).reshape(1)
    order = piece_order(place)
    mult = jnp.exp(logit_scale[0])
    scale = jnp.stack([mult * LOG2E, logit_bias[0] * LOG2E, mult])
    pair = (text_pair % ROWS)[None, :]

    far_txt_feat = exchange(txt_feat, over_y)
    far_img_feat = exchange(img_feat, over_z)
    txt_emb, txt_recip = project(txt_feat, w_txt)
    half = ROWS // 2
    other_lo, other_hi = exchange(txt_emb[:half], over_core), exchange(txt_emb[half:], over_core)
    img_emb, img_recip = project(img_feat, w_img)
    grad_img, grad_txt, grad_other, other_emb, near_loss = near_pairs(
        scale, pair, img_emb, txt_emb, other_lo, other_hi
    )
    (far_txt_feat, far_img_feat, grad_img, grad_txt, grad_other, other_emb, near_loss, slot, order) = (
        lax.optimization_barrier((
            far_txt_feat, far_img_feat, grad_img, grad_txt, grad_other, other_emb, near_loss, slot, order
        ))
    )

    far_txt_emb, far_txt_recip = project(far_txt_feat, w_txt)
    far_other_emb = exchange(far_txt_emb, over_core)
    far_img_emb, far_img_recip = project(far_img_feat, w_img)
    grad_img, grad_far, grad_far_txt, far_send, far_loss = far_text_pairs(
        scale, img_emb, far_img_emb, far_txt_emb, far_other_emb, grad_img
    )
    far_got = exchange(far_send, over_core)
    img_pg, far_img_pg, *bands, grad_txt, send, slab = far_image_pairs(
        scale, img_emb, far_img_emb, txt_emb, other_emb, img_recip, far_img_recip,
        grad_img, grad_far, grad_txt, grad_other, near_loss, far_loss, slot,
    )
    got = exchange(send, over_core)
    slab = slab + exchange(slab, over_core)
    img_got = [exchange(band, over_z) for band in bands]
    far_txt_pg, *bands = far_text_grad(far_txt_emb, far_txt_recip, grad_far_txt, far_got)
    txt_got = [exchange(band, over_y) for band in bands]
    far_txt_pg, img_pg, far_img_pg = lax.optimization_barrier((far_txt_pg, img_pg, far_img_pg))
    img_parts = image_head(order, img_feat, far_img_feat, img_pg, far_img_pg)
    img_keep, img_send = img_parts[:CHAINS], img_parts[CHAINS:]
    img_more = [exchange(part, over_core) for part in img_send]
    txt_pg, *txt_parts = text_head(
        order, txt_feat, far_txt_feat, txt_emb, txt_recip, grad_txt, got, far_txt_pg
    )
    img_more, txt_parts, img_got[0], txt_got[0], slab = lax.optimization_barrier(
        (img_more, txt_parts, img_got[0], txt_got[0], slab)
    )
    txt_keep, txt_send = txt_parts[:CHAINS], txt_parts[CHAINS:]
    txt_more = [exchange(part, over_core) for part in txt_send]

    held = []
    slabs = jnp.broadcast_to(slab, (SEGS, SLAB, PART))
    for chain in range(CHAINS):
        rows = [img_keep[chain] + img_more[chain], txt_keep[chain] + txt_more[chain]]
        held.append(jnp.concatenate(rows + [slabs] * (chain == 0), axis=1))
    both = 2 * SEG_ROWS
    low, high = [None] * CHAINS, [None] * CHAINS
    for chain in range(CHAINS):
        block = held[chain]
        block = block[:2] + over_chain(block[2:], chain, 0)
        block = block[:1] + over_chain(block[1:], chain, 1)
        for step in range(2, len(STEPS)):
            got = over_chain(block, chain, step)
            if chain == 0 and step == 3:
                got, img_got[1], txt_got[1] = lax.optimization_barrier((got, img_got[1], txt_got[1]))
            block = block + got
        if chain == 0:
            loss_sum = jnp.sum(block[0, both:].astype(f32))
            block = block[:, :both]
        got = over_chain(block, chain, 1)
        low[chain] = jnp.concatenate([block, got])
        high[chain] = over_chain(low[chain], chain, 0)
    grad_img_feat = feature_grad(img_pg, img_got, w_img)
    grad_txt_feat = feature_grad(txt_pg, txt_got, w_txt)
    *high, grad_img_feat, grad_txt_feat = lax.optimization_barrier(
        (*high, grad_img_feat, grad_txt_feat)
    )
    own = low + high
    grad_w_img, grad_w_txt = widen(order, *own, *[exchange(part, over_core) for part in own])
    loss_mean = (loss_sum / (ROWS * COUNT * ROUNDS)).reshape(1)
    return (grad_img_feat, grad_txt_feat, grad_w_img, grad_w_txt, loss_mean)


def solution(mesh):
    return jax.shard_map(
        per_device,
        mesh=mesh,
        in_specs=(
            P(("dp", "inner"), None),
            P(("dp", "inner"), None),
            P(("dp", "inner")),
            P(),
            P(),
            P(),
            P(),
        ),
        out_specs=(P(("dp", "inner"), None), P(("dp", "inner"), None), P(), P(), P()),
        check_vma=False,
    )
```
